256 devices in a mesh: tunnel: 32 (over x_hi, z, core), cross: 8 (over x_lo, y).
Axes of the slice: x: 4 (x_hi: 2, x_lo: 2; x = x_hi * 2 + x_lo), y: 4, z: 8, core: 2. Of those that a mesh axis runs over, the one named last changes fastest.
Arguments:
- smoke_air_quantities: float32 [5, 64, 64, 4096], P(None, 'cross', None, 'tunnel'), may hold values from -6 to 6
- lining_state: float32 [3, 16, 256, 4096], P(None, None, 'cross', 'tunnel'), may hold values from -6 to 6
- velocity: float32 [64, 64, 4096], P('cross', None, 'tunnel'), may hold values from 0.1 to 0.5
- diffusion: float32 [5], replicated, may hold values from 0.02 to 0.08
- yields: float32 [5], replicated, may hold values from 0.3 to 3
- rates: float32 [8], replicated, may hold values from 0.05 to 0.15
- fire_cells: int32 [256], replicated, may hold values from 0 to 16777215
- release: float32 [256], replicated, may hold values from 0.5 to 5
- face_cells: int32 [20480], P(('tunnel', 'cross')), may hold values from 0 to 511, as said below
- face_cycle: int32 [20480], P(('tunnel', 'cross')), may hold values from 0 to 255, as said below
- face_count: int32 [256], P(('tunnel', 'cross')), may hold values from 14 to 80, as said below
Outputs:
- fire_out: float32 [5, 64, 64, 4096], P(None, 'cross', None, 'tunnel')
- lining_out: float32 [3, 16, 256, 4096], P(None, None, 'cross', 'tunnel')
The draws below stay inside these ranges and needn't reach their ends.
Inputs may be any that keep to these rules, and one draw needn't show every extreme that they name: `face_cells`: in each device's block of 80 slots the first face_count entries are the cells h * 64 + w of the device's own height band that touch a side wall, the floor or the roof (a corner cell twice); later slots hold 0. `face_cycle`: cycle cell touched by each face row, in the row's own axial segment. Floor, right wall, roof and left wall follow one another round the cycle, turned by an offset that is the same for all segments. Within one axial segment no two live rows name the same cycle cell. Later slots hold 0. `face_count`: devices whose band has the floor or the roof carry more rows than middle bands.
All inputs are finite; a program needn't handle non-finite values.
Results may differ from the reference program's by a relative error of at most 0.00002.
Values sent between devices are 32-bit elements; how exact they have to be, the bound alone decides.
A program may use at most 128 MiB of HBM per device.

```python
import math
import jax
import jax.numpy as jnp

NF = 5
LD = 16
CH = 8
BREADTH_COUNT = 64
UNIT_SPAN_COUNT = 128
SUBSTEPS = 4
NSRC = 256
NH = 64
NA = 4096
CYCLE = 256
RMAX = 80
GRID = 16777216
N_TUNNEL = 32
N_CROSS = 8


def face_tables(key):
    device_total = N_TUNNEL * N_CROSS
    slot_total = 2 * CH + BREADTH_COUNT
    upward_elevation = CH * N_CROSS
    cycle_total = 2 * BREADTH_COUNT + 2 * upward_elevation
    device_ids = jnp.arange(device_total, dtype=jnp.int32)[:, None]
    cross_band = device_ids % N_CROSS
    slot_ids = jnp.arange(slot_total, dtype=jnp.int32)[None, :]
    is_left = slot_ids < CH
    is_right = (slot_ids >= CH) & (slot_ids < 2 * CH)
    is_floor = (slot_ids >= 2 * CH) & (cross_band == 0)
    is_roof = (slot_ids >= 2 * CH) & (cross_band == N_CROSS - 1)
    usable = is_left | is_right | is_floor | is_roof
    height_local = jnp.where(is_left, slot_ids, jnp.where(is_right, slot_ids - CH, jnp.where(is_floor, 0, CH - 1)))
    breadth_positions = jnp.where(is_left, 0, jnp.where(is_right, BREADTH_COUNT - 1, slot_ids - 2 * CH))
    height_global = cross_band * CH + height_local
    position = jnp.where(is_floor, breadth_positions, jnp.where(is_right, BREADTH_COUNT + height_global, jnp.where(is_roof, BREADTH_COUNT + upward_elevation + (BREADTH_COUNT - 1 - breadth_positions), 2 * BREADTH_COUNT + upward_elevation + (upward_elevation - 1 - height_global))))
    offset = jax.random.randint(jax.random.fold_in(key, 11), (), 0, cycle_total)
    cycle_ids = (position + offset) % cycle_total
    cell_ids = height_local * BREADTH_COUNT + breadth_positions
    scores = jax.random.randint(jax.random.fold_in(key, 12), (device_total, slot_total), 0, 1 << 20) * slot_total + slot_ids
    order_keys = jnp.where(usable, 0, 1 << 29) + scores
    order = jnp.argsort(order_keys, axis=1)
    cell_ids = jnp.take_along_axis(jnp.broadcast_to(cell_ids, order.shape), order, axis=1)
    cycle_ids = jnp.take_along_axis(jnp.broadcast_to(cycle_ids, order.shape), order, axis=1)
    base_count = jnp.sum(usable.astype(jnp.int32), axis=1)
    dropped = jax.random.randint(jax.random.fold_in(key, 13), (device_total,), 0, 3)
    dropped = dropped.at[0].set(0)
    counts = base_count - dropped
    live = slot_ids < counts[:, None]
    cell_ids = jnp.where(live, cell_ids, 0)
    cycle_ids = jnp.where(live, cycle_ids, 0)
    return (cell_ids.reshape(-1).astype(jnp.int32), cycle_ids.reshape(-1).astype(jnp.int32), counts.astype(jnp.int32))


def draw_face_cells(key, part):
    return face_tables(key)[0]


def draw_face_cycle(key, part):
    return face_tables(key)[1]


def draw_face_count(key, part):
    return face_tables(key)[2]


def set_ends(entries, key, low, largest):
    dims = entries.shape
    place = [jax.random.randint(jax.random.fold_in(key, axis), (), 0, dims[axis]) for axis in range(len(dims))]
    entries = entries.at[tuple(place)].set(low)
    longest = dims.index(max(dims))
    place[longest] = (place[longest] + 1) % dims[longest]
    return entries.at[tuple(place)].set(largest)


def block_levels(rng, extent, pieces, low, top_value):
    gain = 1.0
    for dim, shards_of in pieces:
        heights = jax.random.uniform(jax.random.fold_in(jax.random.fold_in(rng, 6), dim), (shards_of,), jnp.float32, low / len(pieces), top_value / len(pieces))
        gain = gain * jnp.repeat(jnp.exp(heights), extent[dim] // shards_of).reshape((-1,) + (1,) * (len(extent) - 1 - dim))
    return gain


def scatter_about(stream_key, dims, scale, most, split=(), held_as=jnp.bfloat16):
    values = jax.random.normal(stream_key, dims, jnp.float32) * scale
    if len(split) > 0:
        values = block_levels(stream_key, dims, split, -0.22, 0.18) * values
    return jnp.clip(values, min=-most, max=most).astype(held_as)


def setup_inputs(seed: int = 0) -> dict:
    splits = jax.random.split(jax.random.key(seed), 12)
    smoke_air_quantities = scatter_about(splits[0], (NF, NH, BREADTH_COUNT, NA), 1.0, 6.0, ((1, 8), (3, 32)), jnp.float32)
    lining_state = scatter_about(splits[1], (3, LD, CYCLE, NA), 1.0, 6.0, ((2, 8), (3, 32)), jnp.float32)
    velocity = jnp.clip(0.1 + 0.4 * jax.random.uniform(splits[2], (NH, BREADTH_COUNT, NA), jnp.float32) ** block_levels(splits[2], (NH, BREADTH_COUNT, NA), ((0, 8), (2, 32)), -0.2, 0.2), 0.1, 0.5)
    diffusion = jnp.clip(jnp.exp(jax.random.uniform(splits[3], (NF,), jnp.float32, math.log(0.02), math.log(0.08))), 0.02, 0.08)
    yields = jnp.clip(jnp.exp(jax.random.uniform(splits[4], (NF,), jnp.float32, math.log(0.3), math.log(3.0))), 0.3, 3.0)
    rates = jnp.clip(jnp.exp(jax.random.uniform(splits[5], (8,), jnp.float32, math.log(0.05), math.log(0.15))), 0.05, 0.15)
    fire_cells = set_ends(jax.random.randint(splits[6], (NSRC,), 0, GRID), jax.random.fold_in(splits[6], 1), 0, GRID - 1).astype(jnp.int32)
    release = jnp.clip(jnp.exp(jax.random.uniform(splits[7], (NSRC,), jnp.float32, math.log(0.5), math.log(5.0))), 0.5, 5.0)
    face_cells = draw_face_cells(jax.random.fold_in(splits[11], 71), 0)
    face_cycle = draw_face_cycle(jax.random.fold_in(splits[11], 71), 0)
    face_count = draw_face_count(jax.random.fold_in(splits[11], 71), 0)
    return {"smoke_air_quantities": smoke_air_quantities, "lining_state": lining_state, "velocity": velocity, "diffusion": diffusion, "yields": yields, "rates": rates, "fire_cells": fire_cells, "release": release, "face_cells": face_cells, "face_cycle": face_cycle, "face_count": face_count}


RATE_SCALE = (2.0, 2.0, 1.0, 1.0, 1.0, 1.0, 4.0, 4.0)
FIELD_SIGN = (1.0, 1.0, -1.0, 1.0, 1.0)


def advance_fire(smoke_air_quantities, padded, velocity, diffusion, signed_yields, burn_rate, fuel_source, wall_loss):
    neighbours = (padded[:, 2:, 1:-1, 1:-1] + padded[:, :-2, 1:-1, 1:-1]
                  + padded[:, 1:-1, 2:, 1:-1] + padded[:, 1:-1, :-2, 1:-1]
                  + padded[:, 1:-1, 1:-1, 2:] + padded[:, 1:-1, 1:-1, :-2])
    upstream = padded[:, 1:-1, 1:-1, :-2]
    reaction = burn_rate * smoke_air_quantities[2]
    updated = (smoke_air_quantities - velocity[None] * (smoke_air_quantities - upstream)
               + diffusion[:, None, None, None] * (neighbours - 6.0 * smoke_air_quantities)
               + signed_yields[:, None, None, None] * reaction[None])
    updated = updated.at[2].add(fuel_source)
    return updated.at[0].add(-wall_loss)


def advance_lining(lining_state, cycle_sum, axial_sum, conduct, evap_rate, latent_heat, surface_gain):
    deeper = jnp.concatenate([lining_state[:, 1:], lining_state[:, -1:]], axis=1)
    shallower = jnp.concatenate([lining_state[:, :1], lining_state[:, :-1]], axis=1)
    laplace = deeper + shallower + cycle_sum + axial_sum - 6.0 * lining_state
    evaporation = evap_rate * lining_state[1] * jax.nn.softplus(lining_state[0])
    phase_terms = jnp.stack([-latent_heat * evaporation, -evaporation, evaporation])
    updated = lining_state + conduct[:, None, None, None] * laplace + phase_terms
    return updated.at[0, 0].add(surface_gain)


def reference(smoke_air_quantities, lining_state, velocity, diffusion, yields, rates, fire_cells, release, face_cells, face_cycle, face_count):
    scales = rates * jnp.array(RATE_SCALE, jnp.float32)
    signed_yields = yields * jnp.array(FIELD_SIGN, jnp.float32)
    conduct = scales[3:6]
    upward_elevation = CH * N_CROSS
    length = UNIT_SPAN_COUNT * N_TUNNEL
    fuel_source = jnp.zeros((upward_elevation * BREADTH_COUNT * length,), jnp.float32).at[fire_cells].add(release).reshape(upward_elevation, BREADTH_COUNT, length)
    cell_table = face_cells.reshape(N_TUNNEL, N_CROSS, RMAX)
    cycle_table = face_cycle.reshape(N_TUNNEL, N_CROSS, RMAX)
    count_table = face_count.reshape(N_TUNNEL, N_CROSS)
    live_rows = (jnp.arange(RMAX, dtype=jnp.int32)[None, None, :] < count_table[:, :, None]).astype(jnp.float32)
    band_ids = jnp.arange(N_CROSS, dtype=jnp.int32)[None, :, None]
    portion_positions = jnp.broadcast_to(jnp.arange(N_TUNNEL, dtype=jnp.int32)[:, None, None], cell_table.shape)
    elevation_positions = band_ids * CH + cell_table // BREADTH_COUNT
    breadth_positions = cell_table % BREADTH_COUNT
    for substep in range(SUBSTEPS):
        thermal_excess = smoke_air_quantities[0].reshape(upward_elevation, BREADTH_COUNT, N_TUNNEL, UNIT_SPAN_COUNT)
        air_volume_lines = thermal_excess[elevation_positions, breadth_positions, portion_positions]
        surface = lining_state[0, 0].reshape(CYCLE, N_TUNNEL, UNIT_SPAN_COUNT)
        wall_rows = surface[cycle_table, portion_positions]
        flux = scales[1] * (air_volume_lines - wall_rows) * live_rows[..., None]
        wall_loss = jnp.zeros((upward_elevation, BREADTH_COUNT, N_TUNNEL, UNIT_SPAN_COUNT), jnp.float32).at[elevation_positions, breadth_positions, portion_positions].add(flux).reshape(upward_elevation, BREADTH_COUNT, length)
        surface_gain = jnp.zeros((CYCLE, N_TUNNEL, UNIT_SPAN_COUNT), jnp.float32).at[cycle_table, portion_positions].add(scales[2] * flux).reshape(CYCLE, length)
        padded = jnp.pad(smoke_air_quantities, ((0, 0), (1, 1), (1, 1), (1, 1)))
        fire_next = advance_fire(smoke_air_quantities, padded, velocity, diffusion, signed_yields, scales[0], fuel_source, wall_loss)
        cycle_sum = jnp.roll(lining_state, 1, axis=2) + jnp.roll(lining_state, -1, axis=2)
        axial = jnp.pad(lining_state, ((0, 0), (0, 0), (0, 0), (1, 1)))
        axial_sum = axial[..., 2:] + axial[..., :-2]
        lining_state = advance_lining(lining_state, cycle_sum, axial_sum, conduct, scales[6], scales[7], surface_gain)
        smoke_air_quantities = fire_next
    return smoke_air_quantities, lining_state
```

```python
import jax
import jax.numpy as jnp
from jax import lax
from jax.experimental import pallas as pl
from jax.experimental.pallas import tpu as pltpu
from jax.sharding import PartitionSpec as P

SUBSTEPS = 4
NF = 5
CH = 8
BW = 64
SEG = 128
LD = 16
ARC = 32
NBLK = 3 * LD
NT = 32
NC = 8
ROWS = 80
FIELD_SIGN = (1.0, 1.0, -1.0, 1.0, 1.0)
ORDER = (2, 1, 3, 4, 0)
F32 = jnp.float32
BF16 = jnp.bfloat16
HI = lax.Precision.HIGHEST


def iota(shape, dim):
    return lax.broadcasted_iota(jnp.int32, shape, dim)


def dot_nt(a, b):
    return lax.dot_general(a, b, (((1,), (1,)), ((), ())), preferred_element_type=F32)


def kernel(
    gas, lin, vel, dif, yld, rat, fcell, frel, fcl, fcy, fcn,
    out_gas, out_lin,
    S, L, V, FS, WM, GP, GL, GR, LP, LL, LR, CU, CD, HD, HU, TL, TG, TB, CM, NM, HM, NK,
    ys, yr, xs, xr, cs, cr, ls, lr, tls, tlr, tgs, tgr, tes, ter, tbs, tbr, loc, outs,
):
    t = lax.axis_index("tunnel")
    c = lax.axis_index("cross")
    xl = c // 4
    y = c % 4
    not_bottom = c > 0
    not_top = c < NC - 1
    not_first = t > 0
    not_last = t < NT - 1
    is_end = (c == 0) | (c == NC - 1)
    up = (t, (c + 1) % NC)
    down = (t, (c + NC - 1) % NC)
    right = (t + 1, c)
    left = (t - 1, c)
    column = [(t, xl * 4 + (y + k) % 4) for k in (1, 2, 3)]
    across = (t, (c + 4) % NC)
    edge_row = jnp.where(c == NC - 1, CH, 1)
    lane = iota((8, SEG), 1)
    pair = lane // 2
    odd = lane % 2 == 1
    lane64 = iota((BW, SEG), 1)
    lane32 = iota((ARC, SEG), 1)

    def remote(src, dst, ssem, rsem, dev):
        return pltpu.make_async_remote_copy(
            src_ref=src, dst_ref=dst, send_sem=ssem, recv_sem=rsem,
            device_id=dev, device_id_type=pl.DeviceIdType.MESH,
        )

    mid = pl.ds(8, BW)

    def y_up(s, f):
        return remote(S.at[s, f, CH, mid], S.at[s, f, 0, mid], ys.at[s, f, 0], yr.at[s, f, 0], up)

    def y_down(s, f):
        return remote(S.at[s, f, 1, mid], S.at[s, f, CH + 1, mid], ys.at[s, f, 1], yr.at[s, f, 1], down)

    def x_right(s, f):
        return remote(GP.at[s, f], GL.at[s, f], xs.at[s, f, 0], xr.at[s, f, 0], right)

    def x_left(s, f):
        return remote(GP.at[s, f], GR.at[s, f], xs.at[s, f, 1], xr.at[s, f, 1], left)

    def c_up(s):
        return remote(CU.at[s], HD.at[s], cs.at[s, 0], cr.at[s, 0], up)

    def c_down(s):
        return remote(CD.at[s], HU.at[s], cs.at[s, 1], cr.at[s, 1], down)

    def l_right(s):
        return remote(LP.at[s], LL.at[s], ls.at[s, 0], lr.at[s, 0], right)

    def l_left(s):
        return remote(LP.at[s], LR.at[s], ls.at[s, 1], lr.at[s, 1], left)

    def tl_y(s, k):
        part = TL.at[s, pl.ds(pl.multiple_of(c * ARC, ARC), ARC)]
        return remote(part, part, tls.at[s, k], tlr.at[s, k], column[k])

    def tl_x(s):
        part = TL.at[s, pl.ds(pl.multiple_of(xl * 128, 128), 128)]
        return remote(part, part, tls.at[s, 3], tlr.at[s, 3], across)

    def tg_y(s, k):
        part = TG.at[s, pl.ds(pl.multiple_of(c * 16, 16), 16)]
        return remote(part, part, tgs.at[s, k], tgr.at[s, k], column[k])

    def tg_x(s):
        part = TG.at[s, pl.ds(pl.multiple_of(xl * 64, 64), 64)]
        return remote(part, part, tgs.at[s, 3], tgr.at[s, 3], across)

    def edge_part(s):
        return TG.at[s, pl.ds(pl.multiple_of(128 + xl * 64, 64), 64)]

    def te_y(s, k):
        return remote(edge_part(s), edge_part(s), tes.at[s, k], ter.at[s, 0], column[k])

    def te_x(s):
        return remote(edge_part(s), edge_part(s), tes.at[s, 3], ter.at[s, 1], across)

    def tb_y(k):
        return remote(TB.at[c], TB.at[c], tbs.at[k], tbr.at[k], column[k])

    def tb_x():
        part = TB.at[pl.ds(xl * 4, 4)]
        return remote(part, part, tbs.at[3], tbr.at[3], across)

    def guarded(cond, copy, act):
        @pl.when(cond)
        def _():
            getattr(copy(), act)()

    def y_pair(s, f, act):
        guarded(not_top if act != "wait_recv" else not_bottom, lambda: y_up(s, f), act)
        guarded(not_bottom if act != "wait_recv" else not_top, lambda: y_down(s, f), act)

    def x_pair(s, f, act):
        guarded(not_last if act != "wait_recv" else not_first, lambda: x_right(s, f), act)
        guarded(not_first if act != "wait_recv" else not_last, lambda: x_left(s, f), act)

    def c_pair(s, act):
        getattr(c_up(s), act)()
        getattr(c_down(s), act)()

    def l_pair(s, act):
        guarded(not_last if act != "wait_recv" else not_first, lambda: l_right(s), act)
        guarded(not_first if act != "wait_recv" else not_last, lambda: l_left(s), act)

    def tl_column(s, act):
        for k in range(3):
            getattr(tl_y(s, k), act)()

    def tg_column(s, act):
        for k in range(3):
            getattr(tg_y(s, k), act)()
        if act == "wait_recv":
            guarded(jnp.logical_not(is_end), lambda: te_y(s, 0), act)
        else:
            @pl.when(is_end)
            def _():
                for k in range(3):
                    getattr(te_y(s, k), act)()

    def load_gas(f):
        return pltpu.make_async_copy(gas.at[f], S.at[0, f, pl.ds(1, CH), mid], loc.at[f])

    def load_lin():
        return pltpu.make_async_copy(lin, L.at[0, :, pl.ds(8, ARC)], loc.at[5])

    def load_vel():
        return pltpu.make_async_copy(vel, V, loc.at[6])

    def store_gas(f):
        return pltpu.make_async_copy(S.at[SUBSTEPS, f, pl.ds(1, CH), mid], out_gas.at[f], outs.at[f])

    def store_lin():
        return pltpu.make_async_copy(L.at[SUBSTEPS, :, pl.ds(8, ARC)], out_lin, outs.at[5])

    barrier = pltpu.get_barrier_semaphore()

    def greet(dev):
        pl.semaphore_signal(barrier, inc=1, device_id=dev, device_id_type=pl.DeviceIdType.MESH)

    for dev in column:
        greet(dev)
    greet(across)
    pl.when(y == 3)(lambda: greet(up))
    pl.when(y == 0)(lambda: greet(down))
    pl.when(not_last)(lambda: greet(right))
    pl.when(not_first)(lambda: greet(left))

    for f in ORDER:
        load_gas(f).start()
    load_lin().start()
    load_vel().start()

    zero_rows = jnp.zeros((8, SEG), F32)
    zero_band = jnp.zeros((BW, SEG), F32)

    @pl.loop(0, SUBSTEPS)
    def _(s):
        @pl.loop(0, NF)
        def _(f):
            @pl.loop(1, CH + 1)
            def _(h):
                S[s, f, h, 0:8, :] = zero_rows
                S[s, f, h, 72:80, :] = zero_rows

            @pl.when(c == 0)
            def _():
                S[s, f, 0, mid, :] = zero_band

            @pl.when(c == NC - 1)
            def _():
                S[s, f, CH + 1, mid, :] = zero_band

            @pl.when(t == 0)
            def _():
                GL[s, f] = zero_rows

            @pl.when(t == NT - 1)
            def _():
                GR[s, f] = zero_rows

        @pl.loop(0, 3)
        def _(f):
            @pl.when(t == 0)
            def _():
                LL[s, f] = zero_rows

            @pl.when(t == NT - 1)
            def _():
                LR[s, f] = zero_rows

    @pl.loop(0, CH)
    def _(h):
        WM[h] = zero_band

    live = iota((1, ROWS), 1) < fcn[0]
    TB[c] = jnp.full((8, SEG), -1.0, F32)
    TB[c, 0:1, 0:ROWS] = jnp.where(live, fcl[...], -1).astype(F32)
    TB[c, 1:2, 0:ROWS] = jnp.where(live, fcy[...], -1).astype(F32)

    def side_cell(r):
        return jnp.where(r < CH, r * BW, (r - CH) * BW + BW - 1)

    def edge_cell(h, w):
        return jnp.where((w > 0) & (w < BW - 1), h * BW + w, -2)

    slot = iota((ROWS, SEG), 0)
    own_cell = jnp.where(
        slot < 16,
        side_cell(slot),
        jnp.where(is_end, edge_cell(edge_row - 1, slot - 16), -2),
    ).astype(F32)
    rows_of = (own_cell == TB[c, 0:1, :]).astype(F32)
    cycle_of = (iota((256, SEG), 0).astype(F32) == TB[c, 1:2, :]).astype(BF16)
    CM[...] = dot_nt(rows_of.astype(BF16), cycle_of)
    NM[...] = jnp.broadcast_to(jnp.sum(rows_of, axis=1, keepdims=True), (ROWS, SEG))

    cells = fcell[...]
    hw = cells // 4096 - c * (CH * BW)
    ax = cells % 4096 - t * SEG
    rel = frel[...]
    rel_a = rel.astype(BF16).astype(F32)
    rel_b = (rel - rel_a).astype(BF16).astype(F32)
    rel_c = rel - rel_a - rel_b
    axial_hot = (iota((SEG, 256), 0) == ax).astype(BF16)

    @pl.loop(0, CH)
    def _(h):
        hot = iota((BW, 256), 0) + h * BW == hw
        total = jnp.zeros((BW, SEG), F32)
        for part in (rel_a, rel_b, rel_c):
            total += dot_nt(jnp.where(hot, part, 0.0).astype(BF16), axial_hot)
        FS[h] = total

    def packed_row(block, idx, acc):
        return jnp.where(pair == idx, pltpu.roll(block, 2 * idx + 1, 1), acc)

    def opened(packed, idxs):
        return jnp.concatenate([pltpu.roll(packed, 127 - 2 * i, 1) for i in idxs], axis=0)

    def pack_band(row, h, acc):
        for wg in range(8):
            acc = packed_row(row[8 * wg:8 * wg + 8], 8 * wg + h, acc)
        return acc

    def pack_arc(block, i, acc):
        for g in range(4):
            acc = packed_row(block[8 * g:8 * g + 8], 4 * i + g, acc)
        return acc

    for f in ORDER:
        load_gas(f).wait()
        GP[0, f] = lax.fori_loop(
            0, CH, lambda h, acc: pack_band(S[0, f, h + 1, mid, :], h, acc), zero_rows
        )
    load_lin().wait()
    load_vel().wait()

    def lining_margins(s, b, block):
        CD[s, pl.ds(b, 1), :] = block[0:1]
        CU[s, pl.ds(b, 1), :] = block[ARC - 1:ARC]

    def first_arcs(i, accs):
        new = []
        for f in range(3):
            b = f * LD + i
            block = L[0, b, pl.ds(8, ARC), :]
            lining_margins(0, b, block)
            new.append(pack_arc(block, i, accs[f]))
        return tuple(new)

    accs = lax.fori_loop(0, LD, first_arcs, (zero_rows,) * 3)
    for f in range(3):
        LP[0, f] = accs[f]

    def own_surface(s):
        TL[s, pl.ds(pl.multiple_of(c * ARC, ARC), ARC), :] = L[s, 0, pl.ds(8, ARC), :]

    def own_walls(s):
        sides = [S[s, 0, h + 1, 8:9, :] for h in range(CH)]
        sides += [S[s, 0, h + 1, 71:72, :] for h in range(CH)]
        TG[s, pl.ds(pl.multiple_of(c * 16, 16), 16), :] = jnp.concatenate(sides, axis=0)

        @pl.when(is_end)
        def _():
            TG[s, pl.ds(pl.multiple_of(128 + xl * 64, 64), 64), :] = S[s, 0, edge_row, mid, :]

    own_surface(0)
    own_walls(0)

    pl.semaphore_wait(
        barrier,
        4 + jnp.where((y == 0) | (y == 3), 1, 0) + jnp.where(not_last, 1, 0) + jnp.where(not_first, 1, 0),
    )

    for f in ORDER:
        x_pair(0, f, "start")
    l_pair(0, "start")
    y_pair(0, ORDER[0], "start")
    for k in range(3):
        tb_y(k).start()
    tl_column(0, "start")
    tg_column(0, "start")
    for f in ORDER[1:4]:
        y_pair(0, f, "start")
    c_pair(0, "start")
    y_pair(0, ORDER[4], "start")

    burn = rat[0] * 2.0
    h_wall = rat[1] * 2.0
    gain_rate = rat[2] * h_wall
    evap = rat[6] * 4.0
    latent = rat[7] * 4.0

    def gas_slot(s, f):
        s1 = s + 1
        x_pair(s, f, "wait_recv")
        y_pair(s, f, "wait_recv")
        halo = jnp.where(odd, GR[s, f], GL[s, f])
        d = dif[f]
        react = yld[f] * burn * FIELD_SIGN[f]

        def band(h, acc):
            q = S[s, f, h + 1, mid, :]
            ends = opened(halo, [8 * wg + h for wg in range(8)])
            before = pltpu.roll(jnp.where(lane64 == SEG - 1, ends, q), 1, 1)
            after = pltpu.roll(jnp.where(lane64 == 0, ends, q), SEG - 1, 1)
            around = (
                S[s, f, h + 2, mid, :] + S[s, f, h, mid, :]
                + S[s, f, h + 1, 9:73, :] + S[s, f, h + 1, 7:71, :]
                + after + before
            )
            fuel = q if f == 2 else S[s, 2, h + 1, mid, :]
            new = q - V[h] * (q - before) + d * (around - 6.0 * q) + react * fuel
            if f == 2:
                new = new + FS[h]
            if f == 0:
                new = new - WM[h]
            S[s1, f, h + 1, mid, :] = new
            return pack_band(new, h, acc)

        acc = band(0, zero_rows)
        acc = band(CH - 1, acc)

        @pl.when(s1 < SUBSTEPS)
        def _():
            y_pair(s1, f, "start")

        acc = lax.fori_loop(1, CH - 1, band, acc)

        @pl.when(s1 < SUBSTEPS)
        def _():
            GP[s1, f] = acc
            x_pair(s1, f, "start")

        @pl.when(s1 == SUBSTEPS)
        def _():
            store_gas(f).start()

    def wall_fluxes(s):
        tl_x(s).wait_recv()
        seen = lax.dot_general(
            CM[...], TL[s], (((1,), (0,)), ((), ())), precision=HI, preferred_element_type=F32
        )
        sides = h_wall * (NM[0:16, :] * TG[s, pl.ds(pl.multiple_of(c * 16, 16), 16), :] - seen[0:16])
        rim = h_wall * (NM[16:ROWS, :] * S[s, 0, edge_row, mid, :] - seen[16:ROWS])

        @pl.when(is_end)
        def _():
            WM[edge_row - 1] = rim

        for h in range(CH):
            WM[h, 0:1, :] = sides[h:h + 1]
            WM[h, BW - 1:BW, :] = sides[CH + h:CH + h + 1]

    def lining_tables():
        tb_x().wait_recv()
        r = iota((256, SEG), 0)
        k = (iota((ARC, SEG), 0) + c * ARC).astype(F32)

        def add(b, total):
            cell = jnp.where(
                r < 128,
                jnp.where(r // 16 == b, side_cell(r % 16), -2),
                jnp.where(
                    r < 192,
                    jnp.where(b == 0, edge_cell(0, r - 128), -2),
                    jnp.where(b == NC - 1, edge_cell(CH - 1, r - 192), -2),
                ),
            ).astype(F32)
            rows = (cell == TB[b, 0:1, :]).astype(BF16)
            mine = (k == TB[b, 1:2, :]).astype(BF16)
            return total + dot_nt(mine, rows)

        total = lax.fori_loop(0, NC, add, jnp.zeros((ARC, 256), F32))
        HM[...] = total
        NK[...] = jnp.broadcast_to(jnp.sum(total, axis=1, keepdims=True), (ARC, SEG))

    def lining_slot(s):
        s1 = s + 1
        pl.when(s == 0)(lining_tables)
        tg_x(s).wait_recv()
        te_x(s).wait_recv()
        heat = lax.dot_general(
            HM[...], TG[s], (((1,), (0,)), ((), ())), precision=HI, preferred_element_type=F32
        )
        gain = gain_rate * (heat - NK[...] * L[s, 0, pl.ds(8, ARC), :])
        l_pair(s, "wait_recv")
        c_pair(s, "wait_recv")
        halos = [jnp.where(odd, LR[s, f], LL[s, f]) for f in range(3)]

        def layer(i, accs):
            deep = jnp.minimum(i + 1, LD - 1)
            shallow = jnp.maximum(i - 1, 0)
            old, grown = [], []
            for f in range(3):
                b = f * LD + i
                L[s, b, 7:8, :] = HD[s, pl.ds(b, 1), :]
                L[s, b, 40:41, :] = HU[s, pl.ds(b, 1), :]
                q = L[s, b, pl.ds(8, ARC), :]
                ends = opened(halos[f], [4 * i + g for g in range(4)])
                before = pltpu.roll(jnp.where(lane32 == SEG - 1, ends, q), 1, 1)
                after = pltpu.roll(jnp.where(lane32 == 0, ends, q), SEG - 1, 1)
                around = (
                    L[s, f * LD + deep, pl.ds(8, ARC), :] + L[s, f * LD + shallow, pl.ds(8, ARC), :]
                    + L[s, b, 9:41, :] + L[s, b, 7:39, :] + after + before
                )
                old.append(q)
                grown.append(q + rat[3 + f] * (around - 6.0 * q))
            heat_now, damp, _ = old
            soft = jnp.maximum(heat_now, 0.0) + jnp.log1p(jnp.exp(-jnp.abs(heat_now)))
            e = evap * damp * soft
            new = [
                grown[0] - latent * e + jnp.where(i == 0, gain, 0.0),
                grown[1] - e,
                grown[2] + e,
            ]
            out = []
            for f in range(3):
                b = f * LD + i
                L[s1, b, pl.ds(8, ARC), :] = new[f]
                lining_margins(s1, b, new[f])
                out.append(pack_arc(new[f], i, accs[f]))
            return tuple(out)

        accs = lax.fori_loop(0, LD, layer, (zero_rows,) * 3)

        @pl.when(s1 < SUBSTEPS)
        def _():
            c_pair(s1, "start")
            for f in range(3):
                LP[s1, f] = accs[f]
            l_pair(s1, "start")
            own_surface(s1)
            tl_column(s1, "start")

        @pl.when(s1 == SUBSTEPS)
        def _():
            store_lin().start()

    @pl.loop(0, SUBSTEPS)
    def _(s):
        gas_slot(s, ORDER[0])

        @pl.when(s == 0)
        def _():
            for k in range(3):
                tb_y(k).wait_recv()
            tb_x().start()

        tl_column(s, "wait_recv")
        tl_x(s).start()
        gas_slot(s, ORDER[1])
        tg_column(s, "wait_recv")
        tg_x(s).start()
        te_x(s).start()
        gas_slot(s, ORDER[2])
        gas_slot(s, ORDER[3])
        lining_slot(s)
        wall_fluxes(s)
        gas_slot(s, ORDER[4])

        @pl.when(s + 1 < SUBSTEPS)
        def _():
            own_walls(s + 1)
            tg_column(s + 1, "start")

    for k in range(3):
        tb_y(k).wait_send()
    tb_x().wait_send()

    @pl.loop(0, SUBSTEPS)
    def _(s):
        for f in range(NF):
            x_pair(s, f, "wait_send")
            y_pair(s, f, "wait_send")
        l_pair(s, "wait_send")
        c_pair(s, "wait_send")
        tl_column(s, "wait_send")
        tl_x(s).wait_send()
        tg_column(s, "wait_send")
        tg_x(s).wait_send()
        te_x(s).wait_send()

    for f in ORDER:
        store_gas(f).wait()
    store_lin().wait()


def on_device(gas, lining, velocity, diffusion, yields, rates, fire_cells, release, face_cells, face_cycle, face_count):
    lin = lining.reshape(NBLK, ARC, SEG)
    any_ = pl.BlockSpec(memory_space=pl.ANY)
    smem = pl.BlockSpec(memory_space=pltpu.SMEM)
    vmem = pl.BlockSpec(memory_space=pltpu.VMEM)
    dma = pltpu.SemaphoreType.DMA
    n = SUBSTEPS
    out_gas, out_lin = pl.pallas_call(
        kernel,
        out_shape=(
            jax.ShapeDtypeStruct((NF, CH, BW, SEG), F32),
            jax.ShapeDtypeStruct((NBLK, ARC, SEG), F32),
        ),
        in_specs=[any_, any_, any_, smem, smem, smem, vmem, vmem, vmem, vmem, smem],
        out_specs=(any_, any_),
        scratch_shapes=[
            pltpu.VMEM((n + 1, NF, CH + 2, 80, SEG), F32),
            pltpu.VMEM((n + 1, NBLK, 48, SEG), F32),
            pltpu.VMEM((CH, BW, SEG), F32),
            pltpu.VMEM((CH, BW, SEG), F32),
            pltpu.VMEM((CH, BW, SEG), F32),
            pltpu.VMEM((n, NF, 8, SEG), F32),
            pltpu.VMEM((n, NF, 8, SEG), F32),
            pltpu.VMEM((n, NF, 8, SEG), F32),
            pltpu.VMEM((n, 3, 8, SEG), F32),
            pltpu.VMEM((n, 3, 8, SEG), F32),
            pltpu.VMEM((n, 3, 8, SEG), F32),
            pltpu.VMEM((n + 1, NBLK, SEG), F32),
            pltpu.VMEM((n + 1, NBLK, SEG), F32),
            pltpu.VMEM((n, NBLK, SEG), F32),
            pltpu.VMEM((n, NBLK, SEG), F32),
            pltpu.VMEM((n, 256, SEG), F32),
            pltpu.VMEM((n, 256, SEG), F32),
            pltpu.VMEM((NC, 8, SEG), F32),
            pltpu.VMEM((ROWS, 256), F32),
            pltpu.VMEM((ROWS, SEG), F32),
            pltpu.VMEM((ARC, 256), F32),
            pltpu.VMEM((ARC, SEG), F32),
            dma((n, NF, 2)), dma((n, NF, 2)),
            dma((n, NF, 2)), dma((n, NF, 2)),
            dma((n, 2)), dma((n, 2)),
            dma((n, 2)), dma((n, 2)),
            dma((n, 4)), dma((n, 4)),
            dma((n, 4)), dma((n, 4)),
            dma((n, 4)), dma((n, 2)),
            dma((4,)), dma((4,)),
            dma((7,)), dma((6,)),
        ],
        compiler_params=pltpu.CompilerParams(
            collective_id=0, has_side_effects=True, vmem_limit_bytes=40 * 1024 * 1024
        ),
    )(
        gas, lin, velocity, diffusion, yields, rates,
        fire_cells.reshape(1, -1), release.reshape(1, -1),
        face_cells.reshape(1, -1), face_cycle.reshape(1, -1), face_count,
    )
    return out_gas, out_lin.reshape(lining.shape)


def solution(mesh):
    in_specs = (
        P(None, "cross", None, "tunnel"),
        P(None, None, "cross", "tunnel"),
        P("cross", None, "tunnel"),
        P(), P(), P(), P(), P(),
        P(("tunnel", "cross")),
        P(("tunnel", "cross")),
        P(("tunnel", "cross")),
    )
    out_specs = (P(None, "cross", None, "tunnel"), P(None, None, "cross", "tunnel"))
    return jax.shard_map(on_device, mesh=mesh, in_specs=in_specs, out_specs=out_specs, check_vma=False)
```

```python
import jax
import jax.numpy as jnp
from jax import lax
from jax.experimental import pallas as pl
from jax.experimental.pallas import tpu as pltpu
from jax.sharding import PartitionSpec as P

SUBSTEPS = 4
NF = 5
CH = 8
BW = 64
SEG = 128
LD = 16
ARC = 32
NBLK = 3 * LD
NT = 32
NC = 8
ROWS = 80
FIELD_SIGN = (1.0, 1.0, -1.0, 1.0, 1.0)
ORDER = (2, 1, 3, 4, 0)
F32 = jnp.float32
BF16 = jnp.bfloat16
INNER_FIRST = True
HI = lax.Precision.HIGHEST


def iota(shape, dim):
    return lax.broadcasted_iota(jnp.int32, shape, dim)


def dot_nt(a, b):
    return lax.dot_general(a, b, (((1,), (1,)), ((), ())), preferred_element_type=F32)


def kernel(
    gas, lin, vel, dif_in, yld_in, rat_in, fcell_in, frel_in, fcl_in, fcy_in, fcn_in,
    out_gas, out_lin,
    S, L, V, FS, WM, GP, GL, GR, LP, LL, LR, CU, CD, HD, HU, TL, TB, CM, CT, NM, HM, PT, NK,
    MSK, TLP, TLR, TGC, TGP, TGQ, TGM, TGE, E, EL, SE, dif, yld, rat, fcn, fcell, frel, fcl, fcy,
    ys, yr, xs, xr, cs, cr, ls, lr, tls, tlr, tgs, tgr, tbs, tbr, loc, outs,
):
    t = lax.axis_index("tunnel")
    c = lax.axis_index("cross")
    not_bottom = c > 0
    not_top = c < NC - 1
    not_first = t > 0
    not_last = t < NT - 1
    is_end = (c == 0) | (c == NC - 1)
    up = (t, (c + 1) % NC)
    down = (t, (c + NC - 1) % NC)
    right = (t + 1, c)
    left = (t - 1, c)
    peers = [(c + k) % NC for k in range(1, NC)]
    origins = [(c + NC - k) % NC for k in range(1, NC)]
    edge_row = jnp.where(c == NC - 1, CH, 1)
    lane = iota((8, SEG), 1)
    pair = lane // 2
    odd = lane % 2 == 1
    lane64 = iota((BW, SEG), 1)
    lane32 = iota((ARC, SEG), 1)

    def remote(src, dst, ssem, rsem, dev):
        return pltpu.make_async_remote_copy(
            src_ref=src, dst_ref=dst, send_sem=ssem, recv_sem=rsem,
            device_id=dev, device_id_type=pl.DeviceIdType.MESH,
        )

    mid = pl.ds(8, BW)

    def y_up(s, f):
        return remote(S.at[s, f, CH, mid], S.at[s, f, 0, mid], ys.at[s, f, 0], yr.at[s, f, 0], up)

    def y_down(s, f):
        return remote(S.at[s, f, 1, mid], S.at[s, f, CH + 1, mid], ys.at[s, f, 1], yr.at[s, f, 1], down)

    def x_right(s, f):
        return remote(GP.at[s, f], GL.at[s, f], xs.at[s, f, 0], xr.at[s, f, 0], right)

    def x_left(s, f):
        return remote(GP.at[s, f], GR.at[s, f], xs.at[s, f, 1], xr.at[s, f, 1], left)

    def c_up(s):
        return remote(CU.at[s], HD.at[s], cs.at[s, 0], cr.at[s, 0], up)

    def c_down(s):
        return remote(CD.at[s], HU.at[s], cs.at[s, 1], cr.at[s, 1], down)

    def l_right(s):
        return remote(LP.at[s], LL.at[s], ls.at[s, 0], lr.at[s, 0], right)

    def l_left(s):
        return remote(LP.at[s], LR.at[s], ls.at[s, 1], lr.at[s, 1], left)

    def at_rim(b):
        return (b == 0) | (b == NC - 1)

    def arc_of(b):
        return pl.ds(pl.multiple_of(b * ARC, ARC), ARC)

    def eight_of(b):
        return pl.ds(pl.multiple_of(b * 8, 8), 8)

    def tl_whole(s, k):
        part = TL.at[s, arc_of(c)]
        return remote(part, part, tls.at[s, k], tlr.at[s, k], (t, peers[k]))

    def tl_placed(s, k):
        return remote(
            TLP.at[s, eight_of(peers[k])], TLR.at[s, eight_of(c)], tls.at[s, k], tlr.at[s, k], (t, peers[k])
        )

    def tg_mid(s, k):
        return remote(
            TGP.at[s, eight_of(peers[k])], TGM.at[s, eight_of(c)], tgs.at[s, k], tgr.at[s, k], (t, peers[k])
        )

    def tg_rim(s, k):
        return remote(
            TGQ.at[s, arc_of(peers[k])], TGE.at[s, c // (NC - 1)], tgs.at[s, k], tgr.at[s, k], (t, peers[k])
        )

    def tb_all(k):
        return remote(TB.at[c], TB.at[c], tbs.at[k], tbr.at[k], (t, peers[k]))

    def guarded(cond, copy, act):
        @pl.when(cond)
        def _():
            getattr(copy(), act)()

    def y_pair(s, f, act):
        guarded(not_top if act != "wait_recv" else not_bottom, lambda: y_up(s, f), act)
        guarded(not_bottom if act != "wait_recv" else not_top, lambda: y_down(s, f), act)

    def x_pair(s, f, act):
        guarded(not_last if act != "wait_recv" else not_first, lambda: x_right(s, f), act)
        guarded(not_first if act != "wait_recv" else not_last, lambda: x_left(s, f), act)

    def c_pair(s, act):
        getattr(c_up(s), act)()
        getattr(c_down(s), act)()

    def l_pair(s, act):
        guarded(not_last if act != "wait_recv" else not_first, lambda: l_right(s), act)
        guarded(not_first if act != "wait_recv" else not_last, lambda: l_left(s), act)

    def either(cond, one, two, act):
        guarded(cond, one, act)
        guarded(jnp.logical_not(cond), two, act)

    def tl_group(s, act):
        for k in range(NC - 1):
            whole = is_end if act == "wait_recv" else at_rim(peers[k])
            either(whole | (s == 0), lambda: tl_whole(s, k), lambda: tl_placed(s, k), act)

    def tg_group(s, act):
        for k in range(NC - 1):
            rim = at_rim(origins[k]) if act == "wait_recv" else is_end
            either(rim, lambda: tg_rim(s, k), lambda: tg_mid(s, k), act)

    def tb_group(act):
        for k in range(NC - 1):
            getattr(tb_all(k), act)()

    def load_gas(f):
        return pltpu.make_async_copy(gas.at[f], S.at[0, f, pl.ds(1, CH), mid], loc.at[f])

    def load_lin():
        return pltpu.make_async_copy(lin, L.at[0, :, pl.ds(8, ARC)], loc.at[5])

    def load_vel():
        return pltpu.make_async_copy(vel, V, loc.at[6])

    def store_gas(f):
        return pltpu.make_async_copy(S.at[SUBSTEPS, f, pl.ds(1, CH), mid], out_gas.at[f], outs.at[f])

    def store_lin():
        return pltpu.make_async_copy(L.at[SUBSTEPS, :, pl.ds(8, ARC)], out_lin, outs.at[5])

    barrier = pltpu.get_barrier_semaphore()

    def greet(dev):
        pl.semaphore_signal(barrier, inc=1, device_id=dev, device_id_type=pl.DeviceIdType.MESH)

    for b in peers:
        greet((t, b))
    pl.when(not_last)(lambda: greet(right))
    pl.when(not_first)(lambda: greet(left))

    small = [
        pltpu.make_async_copy(src, dst, loc.at[7 + i])
        for i, (src, dst) in enumerate(
            ((fcn_in, fcn), (fcl_in, fcl), (fcy_in, fcy), (fcell_in, fcell), (frel_in, frel),
             (dif_in, dif), (yld_in, yld), (rat_in, rat))
        )
    ]
    for copy in small:
        copy.start()
    for f in ORDER:
        load_gas(f).start()
    load_lin().start()
    load_vel().start()

    zero_rows = jnp.zeros((8, SEG), F32)
    zero_band = jnp.zeros((BW, SEG), F32)

    @pl.loop(0, SUBSTEPS)
    def _(s):
        @pl.loop(0, NF)
        def _(f):
            @pl.loop(1, CH + 1)
            def _(h):
                S[s, f, h, 0:8, :] = zero_rows
                S[s, f, h, 72:80, :] = zero_rows

            @pl.when(c == 0)
            def _():
                S[s, f, 0, mid, :] = zero_band

            @pl.when(c == NC - 1)
            def _():
                S[s, f, CH + 1, mid, :] = zero_band

            @pl.when(t == 0)
            def _():
                GL[s, f] = zero_rows

            @pl.when(t == NT - 1)
            def _():
                GR[s, f] = zero_rows

        @pl.loop(0, 3)
        def _(f):
            @pl.when(t == 0)
            def _():
                LL[s, f] = zero_rows

            @pl.when(t == NT - 1)
            def _():
                LR[s, f] = zero_rows

        TGM[s, 0:8, :] = zero_rows
        TGM[s, 56:64, :] = zero_rows

    @pl.loop(0, CH)
    def _(h):
        WM[h] = zero_band

    for copy in small:
        copy.wait()

    live = iota((1, ROWS), 1) < fcn[0]
    TB[c] = jnp.full((8, SEG), -1.0, F32)
    TB[c, 0:1, 0:ROWS] = jnp.where(live, fcl[...], -1).astype(F32)
    TB[c, 1:2, 0:ROWS] = jnp.where(live, fcy[...], -1).astype(F32)

    def side_cell(r):
        return jnp.where(r < CH, r * BW, (r - CH) * BW + BW - 1)

    def edge_cell(h, w):
        return jnp.where((w > 0) & (w < BW - 1), h * BW + w, -2)

    slot = iota((ROWS, SEG), 0)
    own_cell = jnp.where(
        slot < 16,
        side_cell(slot),
        jnp.where(is_end, edge_cell(edge_row - 1, slot - 16), -2),
    ).astype(F32)
    rows_of = (own_cell == TB[c, 0:1, :]).astype(F32)
    cycle_of = (iota((256, SEG), 0).astype(F32) == TB[c, 1:2, :]).astype(BF16)
    CM[...] = dot_nt(rows_of.astype(BF16), cycle_of)
    CT[...] = dot_nt(cycle_of, rows_of.astype(BF16))
    sides_seen = CM[0:16, :].astype(BF16)
    for b in range(NC):
        arc_rows = (iota((256, SEG), 0) // ARC == b).astype(BF16)
        MSK[b] = lax.dot_general(
            sides_seen, arc_rows, (((1,), (0,)), ((), ())), preferred_element_type=F32
        )
    NM[...] = jnp.broadcast_to(jnp.sum(rows_of, axis=1, keepdims=True), (ROWS, SEG))

    cells = fcell[...]
    hw = cells // 4096 - c * (CH * BW)
    ax = cells % 4096 - t * SEG
    rel = frel[...]
    rel_a = rel.astype(BF16).astype(F32)
    rel_b = (rel - rel_a).astype(BF16).astype(F32)
    rel_c = rel - rel_a - rel_b
    axial_hot = (iota((SEG, 256), 0) == ax).astype(BF16)

    @pl.loop(0, CH)
    def _(h):
        hot = iota((BW, 256), 0) + h * BW == hw
        total = jnp.zeros((BW, SEG), F32)
        for part in (rel_a, rel_b, rel_c):
            total += dot_nt(jnp.where(hot, part, 0.0).astype(BF16), axial_hot)
        FS[h] = total

    def open_band(packed, dst):
        for h in range(CH):
            for wg in range(8):
                dst[h, 8 * wg:8 * wg + 8, :] = pltpu.roll(packed, 127 - 2 * (8 * wg + h), 1)

    def pack_band(s, f):
        acc = zero_rows
        for h in range(CH):
            for wg in range(8):
                idx = 8 * wg + h
                rows = S[s, f, h + 1, 8 + 8 * wg:16 + 8 * wg, :]
                acc = jnp.where(pair == idx, pltpu.roll(rows, 2 * idx + 1, 1), acc)
        GP[s, f] = acc

    def open_arc(packed, f):
        for i in range(LD):
            for g in range(4):
                EL[f * LD + i, 8 * g:8 * g + 8, :] = pltpu.roll(packed, 127 - 2 * (4 * i + g), 1)

    def pack_arc(s, f):
        acc = zero_rows
        for i in range(LD):
            for g in range(4):
                idx = 4 * i + g
                rows = L[s, f * LD + i, 8 + 8 * g:16 + 8 * g, :]
                acc = jnp.where(pair == idx, pltpu.roll(rows, 2 * idx + 1, 1), acc)
        LP[s, f] = acc

    def lining_margins(s):
        for b in range(NBLK):
            CD[s, b:b + 1, :] = L[s, b, 8:9, :]
            CU[s, b:b + 1, :] = L[s, b, 39:40, :]

    for f in ORDER:
        load_gas(f).wait()
        pack_band(0, f)
    load_lin().wait()
    load_vel().wait()
    lining_margins(0)
    for f in range(3):
        pack_arc(0, f)

    def own_surface(s):
        TL[s, arc_of(c), :] = L[s, 0, pl.ds(8, ARC), :]

    def own_walls(s):
        for h in range(CH):
            TGC[h:h + 1, :] = S[s, 0, h + 1, 8:9, :]
            TGC[CH + h:CH + h + 1, :] = S[s, 0, h + 1, 71:72, :]

        @pl.when(is_end)
        def _():
            TGC[16:ROWS, :] = S[s, 0, edge_row, mid, :]
            TGQ[s] = lax.dot_general(
                CT[...], TGC[...], (((1,), (0,)), ((), ())), precision=HI, preferred_element_type=F32
            )
            TGE[s, c // (NC - 1)] = TGQ[s, arc_of(c), :]

        @pl.when(jnp.logical_not(is_end))
        def _():
            for b in range(NC):
                TGP[s, 8 * b:8 * b + 8, :] = MSK[b, 0:8] * TGC[0:8, :] + MSK[b, 8:16] * TGC[8:16, :]
            TGM[s, eight_of(c), :] = TGP[s, eight_of(c), :]

    own_surface(0)
    own_walls(0)

    pl.semaphore_wait(
        barrier,
        NC - 1 + jnp.where(not_last, 1, 0) + jnp.where(not_first, 1, 0),
    )

    for f in ORDER:
        x_pair(0, f, "start")
    y_pair(0, ORDER[0], "start")
    tb_group("start")
    tl_group(0, "start")
    for f in ORDER[1:]:
        y_pair(0, f, "start")
    tg_group(0, "start")
    l_pair(0, "start")
    c_pair(0, "start")

    burn = rat[0] * 2.0
    h_wall = rat[1] * 2.0
    gain_rate = rat[2] * h_wall
    evap = rat[6] * 4.0
    latent = rat[7] * 4.0

    def gas_slot(s, f):
        s1 = s + 1
        d = dif[f]
        react = yld[f] * burn * FIELD_SIGN[f]

        def band(h):
            q = S[s, f, h + 1, mid, :]
            ends = E[f, h]
            before = pltpu.roll(jnp.where(lane64 == SEG - 1, ends, q), 1, 1)
            after = pltpu.roll(jnp.where(lane64 == 0, ends, q), SEG - 1, 1)
            around = (
                S[s, f, h + 2, mid, :] + S[s, f, h, mid, :]
                + S[s, f, h + 1, 9:73, :] + S[s, f, h + 1, 7:71, :]
                + after + before
            )
            fuel = q if f == 2 else S[s, 2, h + 1, mid, :]
            new = q - V[h] * (q - before) + d * (around - 6.0 * q) + react * fuel
            if f == 2:
                new = new + FS[h]
            if f == 0:
                new = new - WM[h]
            S[s1, f, h + 1, mid, :] = new

        x_pair(s, f, "wait_recv")
        open_band(jnp.where(odd, GR[s, f], GL[s, f]), E.at[f])
        if INNER_FIRST:
            for h in range(1, CH - 1):
                band(h)
        y_pair(s, f, "wait_recv")
        band(0)
        band(CH - 1)

        @pl.when(s1 < SUBSTEPS)
        def _():
            y_pair(s1, f, "start")

        if not INNER_FIRST:
            for h in range(1, CH - 1):
                band(h)

        @pl.when(s1 < SUBSTEPS)
        def _():
            pack_band(s1, f)
            x_pair(s1, f, "start")

        @pl.when(s1 == SUBSTEPS)
        def _():
            store_gas(f).start()

    def wall_fluxes(s):
        tl_group(s, "wait_recv")
        for h in range(CH):
            TGC[h:h + 1, :] = S[s, 0, h + 1, 8:9, :]
            TGC[CH + h:CH + h + 1, :] = S[s, 0, h + 1, 71:72, :]

        def side_walls(seen):
            sides = h_wall * (NM[0:16, :] * TGC[0:16, :] - seen)
            for h in range(CH):
                WM[h, 0:1, :] = sides[h:h + 1]
                WM[h, BW - 1:BW, :] = sides[CH + h:CH + h + 1]

        @pl.when(is_end | (s == 0))
        def _():
            seen = lax.dot_general(
                CM[...], TL[s], (((1,), (0,)), ((), ())), precision=HI, preferred_element_type=F32
            )

            @pl.when(is_end)
            def _():
                WM[edge_row - 1] = h_wall * (NM[16:ROWS, :] * S[s, 0, edge_row, mid, :] - seen[16:ROWS])

            side_walls(seen[0:16])

        @pl.when(jnp.logical_not(is_end | (s == 0)))
        def _():
            seen = jnp.zeros((16, SEG), F32)
            for b in range(NC):
                rows = TLR[s, 8 * b:8 * b + 8, :]
                seen = seen + MSK[b] * jnp.concatenate([rows, rows], axis=0)
            side_walls(seen)

    def lining_tables():
        tb_group("wait_recv")
        r = iota((8 * NC, SEG), 0)
        k = (iota((ARC, SEG), 0) + c * ARC).astype(F32)

        def add(b, totals):
            heat, placed, count = totals
            here = r // 8 == b
            low = jnp.where(here, r % 8 * BW, -2).astype(F32)
            high = jnp.where(here, r % 8 * BW + BW - 1, -2).astype(F32)
            rows = ((low == TB[b, 0:1, :]) | (high == TB[b, 0:1, :])).astype(BF16)
            mine = (k == TB[b, 1:2, :]).astype(F32)
            hot = mine.astype(BF16)
            inner = (b > 0) & (b < NC - 1)
            heat = heat + jnp.where(inner, dot_nt(hot, rows), 0.0)
            placed = placed + dot_nt(rows, hot)
            return heat, placed, count + jnp.sum(mine, axis=1, keepdims=True)

        heat, placed, count = lax.fori_loop(
            0, NC, add,
            (jnp.zeros((ARC, 8 * NC), F32), jnp.zeros((8 * NC, ARC), F32), jnp.zeros((ARC, 1), F32)),
        )
        HM[...] = heat
        PT[...] = placed
        NK[...] = jnp.broadcast_to(count, (ARC, SEG))

    def lining_slot(s):
        s1 = s + 1
        pl.when(s == 0)(lining_tables)
        tg_group(s, "wait_recv")
        heat = lax.dot_general(
            HM[...], TGM[s], (((1,), (0,)), ((), ())), precision=HI, preferred_element_type=F32
        ) + TGE[s, 0] + TGE[s, 1]
        gain = gain_rate * (heat - NK[...] * L[s, 0, pl.ds(8, ARC), :])
        heat_now = L[s, 0:LD, pl.ds(8, ARC), :]
        soft = jnp.maximum(heat_now, 0.0) + jnp.log1p(jnp.exp(-jnp.abs(heat_now)))
        SE[...] = evap * L[s, LD:2 * LD, pl.ds(8, ARC), :] * soft
        l_pair(s, "wait_recv")
        for f in range(3):
            open_arc(jnp.where(odd, LR[s, f], LL[s, f]), f)
        c_pair(s, "wait_recv")
        for b in range(NBLK):
            L[s, b, 7:8, :] = HD[s, b:b + 1, :]
            L[s, b, 40:41, :] = HU[s, b:b + 1, :]

        def diffused(f, i):
            deep = min(i + 1, LD - 1)
            shallow = max(i - 1, 0)
            b = f * LD + i
            q = L[s, b, pl.ds(8, ARC), :]
            ends = EL[b]
            before = pltpu.roll(jnp.where(lane32 == SEG - 1, ends, q), 1, 1)
            after = pltpu.roll(jnp.where(lane32 == 0, ends, q), SEG - 1, 1)
            around = (
                L[s, f * LD + deep, pl.ds(8, ARC), :] + L[s, f * LD + shallow, pl.ds(8, ARC), :]
                + L[s, b, 9:41, :] + L[s, b, 7:39, :] + after + before
            )
            return q + rat[3 + f] * (around - 6.0 * q)

        L[s1, 0, pl.ds(8, ARC), :] = diffused(0, 0) - latent * SE[0] + gain

        @pl.when(s1 < SUBSTEPS)
        def _():
            own_surface(s1)
            TLP[s1] = lax.dot_general(
                PT[...], L[s1, 0, pl.ds(8, ARC), :], (((1,), (0,)), ((), ())),
                precision=HI, preferred_element_type=F32,
            )
            TLR[s1, eight_of(c), :] = TLP[s1, eight_of(c), :]
            tl_group(s1, "start")

        for i in range(LD):
            e = SE[i]
            if i > 0:
                L[s1, i, pl.ds(8, ARC), :] = diffused(0, i) - latent * e
            L[s1, LD + i, pl.ds(8, ARC), :] = diffused(1, i) - e
            L[s1, 2 * LD + i, pl.ds(8, ARC), :] = diffused(2, i) + e

        @pl.when(s1 < SUBSTEPS)
        def _():
            lining_margins(s1)
            c_pair(s1, "start")
            for f in range(3):
                pack_arc(s1, f)
            l_pair(s1, "start")

        @pl.when(s1 == SUBSTEPS)
        def _():
            store_lin().start()

    @pl.loop(0, SUBSTEPS)
    def _(s):
        for f in ORDER[:4]:
            gas_slot(s, f)
        wall_fluxes(s)
        gas_slot(s, ORDER[4])

        @pl.when(s + 1 < SUBSTEPS)
        def _():
            own_walls(s + 1)
            tg_group(s + 1, "start")

        lining_slot(s)

    tb_group("wait_send")

    @pl.loop(0, SUBSTEPS)
    def _(s):
        for f in range(NF):
            x_pair(s, f, "wait_send")
            y_pair(s, f, "wait_send")
        l_pair(s, "wait_send")
        c_pair(s, "wait_send")
        tl_group(s, "wait_send")
        tg_group(s, "wait_send")

    for f in ORDER:
        store_gas(f).wait()
    store_lin().wait()


def on_device(gas, lining, velocity, diffusion, yields, rates, fire_cells, release, face_cells, face_cycle, face_count):
    lin = lining.reshape(NBLK, ARC, SEG)
    any_ = pl.BlockSpec(memory_space=pl.ANY)
    dma = pltpu.SemaphoreType.DMA
    n = SUBSTEPS
    out_gas, out_lin = pl.pallas_call(
        kernel,
        out_shape=(
            jax.ShapeDtypeStruct((NF, CH, BW, SEG), F32),
            jax.ShapeDtypeStruct((NBLK, ARC, SEG), F32),
        ),
        in_specs=[any_] * 11,
        out_specs=(any_, any_),
        scratch_shapes=[
            pltpu.VMEM((n + 1, NF, CH + 2, 80, SEG), F32),
            pltpu.VMEM((n + 1, NBLK, 48, SEG), F32),
            pltpu.VMEM((CH, BW, SEG), F32),
            pltpu.VMEM((CH, BW, SEG), F32),
            pltpu.VMEM((CH, BW, SEG), F32),
            pltpu.VMEM((n, NF, 8, SEG), F32),
            pltpu.VMEM((n, NF, 8, SEG), F32),
            pltpu.VMEM((n, NF, 8, SEG), F32),
            pltpu.VMEM((n, 3, 8, SEG), F32),
            pltpu.VMEM((n, 3, 8, SEG), F32),
            pltpu.VMEM((n, 3, 8, SEG), F32),
            pltpu.VMEM((n, NBLK, SEG), F32),
            pltpu.VMEM((n, NBLK, SEG), F32),
            pltpu.VMEM((n, NBLK, SEG), F32),
            pltpu.VMEM((n, NBLK, SEG), F32),
            pltpu.VMEM((n, 256, SEG), F32),
            pltpu.VMEM((NC, 8, SEG), F32),
            pltpu.VMEM((ROWS, 256), F32),
            pltpu.VMEM((256, ROWS), F32),
            pltpu.VMEM((ROWS, SEG), F32),
            pltpu.VMEM((ARC, 8 * NC), F32),
            pltpu.VMEM((8 * NC, ARC), F32),
            pltpu.VMEM((ARC, SEG), F32),
            pltpu.VMEM((NC, 16, SEG), F32),
            pltpu.VMEM((n, 8 * NC, SEG), F32),
            pltpu.VMEM((n, 8 * NC, SEG), F32),
            pltpu.VMEM((ROWS, SEG), F32),
            pltpu.VMEM((n, 8 * NC, SEG), F32),
            pltpu.VMEM((n, 256, SEG), F32),
            pltpu.VMEM((n, 8 * NC, SEG), F32),
            pltpu.VMEM((n, 2, ARC, SEG), F32),
            pltpu.VMEM((NF, CH, BW, SEG), F32),
            pltpu.VMEM((NBLK, ARC, SEG), F32),
            pltpu.VMEM((LD, ARC, SEG), F32),
            pltpu.SMEM((NF,), F32),
            pltpu.SMEM((NF,), F32),
            pltpu.SMEM((8,), F32),
            pltpu.SMEM((1,), jnp.int32),
            pltpu.VMEM((1, 256), jnp.int32),
            pltpu.VMEM((1, 256), F32),
            pltpu.VMEM((1, ROWS), jnp.int32),
            pltpu.VMEM((1, ROWS), jnp.int32),
            dma((n, NF, 2)), dma((n, NF, 2)),
            dma((n, NF, 2)), dma((n, NF, 2)),
            dma((n, 2)), dma((n, 2)),
            dma((n, 2)), dma((n, 2)),
            dma((n, NC - 1)), dma((n, NC - 1)),
            dma((n, NC - 1)), dma((n, NC - 1)),
            dma((NC - 1,)), dma((NC - 1,)),
            dma((15,)), dma((6,)),
        ],
        compiler_params=pltpu.CompilerParams(
            collective_id=0, has_side_effects=True, vmem_limit_bytes=56 * 1024 * 1024
        ),
    )(
        gas, lin, velocity, diffusion, yields, rates,
        fire_cells.reshape(1, -1), release.reshape(1, -1),
        face_cells.reshape(1, -1), face_cycle.reshape(1, -1), face_count,
    )
    return out_gas, out_lin.reshape(lining.shape)


def solution(mesh):
    in_specs = (
        P(None, "cross", None, "tunnel"),
        P(None, None, "cross", "tunnel"),
        P("cross", None, "tunnel"),
        P(), P(), P(), P(), P(),
        P(("tunnel", "cross")),
        P(("tunnel", "cross")),
        P(("tunnel", "cross")),
    )
    out_specs = (P(None, "cross", None, "tunnel"), P(None, None, "cross", "tunnel"))
    return jax.shard_map(on_device, mesh=mesh, in_specs=in_specs, out_specs=out_specs, check_vma=False)
```

```python
import jax
import jax.numpy as jnp
from jax import lax
from jax.experimental import pallas as pl
from jax.experimental.pallas import tpu as pltpu
from jax.sharding import PartitionSpec as P

SUBSTEPS = 4
NF = 5
CH = 8
BW = 64
SEG = 128
LD = 16
ARC = 32
NBLK = 3 * LD
NT = 32
NC = 8
ROWS = 80
FIELD_SIGN = (1.0, 1.0, -1.0, 1.0, 1.0)
ORDER = (2, 1, 3, 4, 0)
F32 = jnp.float32
BF16 = jnp.bfloat16
INNER_FIRST = True


def iota(shape, dim):
    return lax.broadcasted_iota(jnp.int32, shape, dim)


def dot_nt(a, b):
    return lax.dot_general(a, b, (((1,), (1,)), ((), ())), preferred_element_type=F32)


def pick(table, rows):
    a = rows.astype(BF16)
    rest = rows - a.astype(F32)
    b = rest.astype(BF16)
    d = (rest - b.astype(F32)).astype(BF16)
    parts = jnp.concatenate([a, b, d], axis=1)
    out = lax.dot_general(table, parts, (((1,), (0,)), ((), ())), preferred_element_type=F32)
    n = rows.shape[1]
    return out[:, 0:n] + out[:, n:2 * n] + out[:, 2 * n:3 * n]


def kernel(
    gas, lin, vel, dif_in, yld_in, rat_in, fcell_in, frel_in, fcl_in, fcy_in, fcn_in,
    out_gas, out_lin,
    S, L, V, FS, WM, GP, GL, GR, LP, LL, LR, CU, CD, HD, HU, TL, TB, CM, CT, NM, HM, PT, NK,
    MSK, TLP, TLR, TGC, TGP, TGQ, TGM, TGE, E, EL, SE, dif, yld, rat, fcn, fcell, frel, fcl, fcy,
    ys, yr, xs, xr, cs, cr, ls, lr, tls, tlr, tgs, tgr, tbs, tbr, loc, outs,
):
    t = lax.axis_index("tunnel")
    c = lax.axis_index("cross")
    not_bottom = c > 0
    not_top = c < NC - 1
    not_first = t > 0
    not_last = t < NT - 1
    is_end = (c == 0) | (c == NC - 1)
    up = (t, (c + 1) % NC)
    down = (t, (c + NC - 1) % NC)
    right = (t + 1, c)
    left = (t - 1, c)
    peers = [(c + k) % NC for k in range(1, NC)]
    origins = [(c + NC - k) % NC for k in range(1, NC)]
    edge_row = jnp.where(c == NC - 1, CH, 1)
    lane = iota((8, SEG), 1)
    pair = lane // 2
    odd = lane % 2 == 1
    lane64 = iota((BW, SEG), 1)
    lane32 = iota((ARC, SEG), 1)

    def remote(src, dst, ssem, rsem, dev):
        return pltpu.make_async_remote_copy(
            src_ref=src, dst_ref=dst, send_sem=ssem, recv_sem=rsem,
            device_id=dev, device_id_type=pl.DeviceIdType.MESH,
        )

    mid = pl.ds(8, BW)

    def y_up(s, f):
        return remote(S.at[s, f, CH, mid], S.at[s, f, 0, mid], ys.at[s, f, 0], yr.at[s, f, 0], up)

    def y_down(s, f):
        return remote(S.at[s, f, 1, mid], S.at[s, f, CH + 1, mid], ys.at[s, f, 1], yr.at[s, f, 1], down)

    def y_first(f, row, side, dev):
        dst = S.at[0, f, (CH + 1) * side, mid]
        return remote(gas.at[f, row], dst, ys.at[0, f, side], yr.at[0, f, side], dev)

    def x_right(s, f):
        return remote(GP.at[s, f], GL.at[s, f], xs.at[s, f, 0], xr.at[s, f, 0], right)

    def x_left(s, f):
        return remote(GP.at[s, f], GR.at[s, f], xs.at[s, f, 1], xr.at[s, f, 1], left)

    def c_up(s):
        return remote(CU.at[s], HD.at[s], cs.at[s, 0], cr.at[s, 0], up)

    def c_down(s):
        return remote(CD.at[s], HU.at[s], cs.at[s, 1], cr.at[s, 1], down)

    def l_right(s):
        return remote(LP.at[s], LL.at[s], ls.at[s, 0], lr.at[s, 0], right)

    def l_left(s):
        return remote(LP.at[s], LR.at[s], ls.at[s, 1], lr.at[s, 1], left)

    def at_rim(b):
        return (b == 0) | (b == NC - 1)

    def arc_of(b):
        return pl.ds(pl.multiple_of(b * ARC, ARC), ARC)

    def eight_of(b):
        return pl.ds(pl.multiple_of(b * 8, 8), 8)

    def tl_whole(s, k):
        part = TL.at[s, arc_of(c)]
        return remote(part, part, tls.at[s, k], tlr.at[s, k], (t, peers[k]))

    def tl_first(k):
        return remote(lin.at[0], TL.at[0, arc_of(c)], tls.at[0, k], tlr.at[0, k], (t, peers[k]))

    def tl_placed(s, k):
        return remote(
            TLP.at[s, eight_of(peers[k])], TLR.at[s, eight_of(c)], tls.at[s, k], tlr.at[s, k], (t, peers[k])
        )

    def tg_mid(s, k):
        return remote(
            TGP.at[s, eight_of(peers[k])], TGM.at[s, eight_of(c)], tgs.at[s, k], tgr.at[s, k], (t, peers[k])
        )

    def tg_rim(s, k):
        return remote(
            TGQ.at[s, arc_of(peers[k])], TGE.at[s, c // (NC - 1)], tgs.at[s, k], tgr.at[s, k], (t, peers[k])
        )

    def tb_all(k):
        return remote(TB.at[c], TB.at[c], tbs.at[k], tbr.at[k], (t, peers[k]))

    def guarded(cond, copy, act):
        @pl.when(cond)
        def _():
            getattr(copy(), act)()

    def y_pair(s, f, act):
        guarded(not_top if act != "wait_recv" else not_bottom, lambda: y_up(s, f), act)
        guarded(not_bottom if act != "wait_recv" else not_top, lambda: y_down(s, f), act)

    def x_pair(s, f, act):
        guarded(not_last if act != "wait_recv" else not_first, lambda: x_right(s, f), act)
        guarded(not_first if act != "wait_recv" else not_last, lambda: x_left(s, f), act)

    def c_pair(s, act):
        getattr(c_up(s), act)()
        getattr(c_down(s), act)()

    def l_pair(s, act):
        guarded(not_last if act != "wait_recv" else not_first, lambda: l_right(s), act)
        guarded(not_first if act != "wait_recv" else not_last, lambda: l_left(s), act)

    def either(cond, one, two, act):
        guarded(cond, one, act)
        guarded(jnp.logical_not(cond), two, act)

    def tl_group(s, act):
        for k in range(NC - 1):
            whole = is_end if act == "wait_recv" else at_rim(peers[k])
            either(whole | (s == 0), lambda: tl_whole(s, k), lambda: tl_placed(s, k), act)

    def tg_group(s, act):
        for k in range(NC - 1):
            rim = at_rim(origins[k]) if act == "wait_recv" else is_end
            either(rim, lambda: tg_rim(s, k), lambda: tg_mid(s, k), act)

    def tb_group(act):
        for k in range(NC - 1):
            getattr(tb_all(k), act)()

    def load_gas(f):
        return pltpu.make_async_copy(gas.at[f], S.at[0, f, pl.ds(1, CH), mid], loc.at[f])

    def load_lin():
        return pltpu.make_async_copy(lin, L.at[0, :, pl.ds(8, ARC)], loc.at[5])

    def load_vel():
        return pltpu.make_async_copy(vel, V, loc.at[6])

    def store_gas(f):
        return pltpu.make_async_copy(S.at[SUBSTEPS, f, pl.ds(1, CH), mid], out_gas.at[f], outs.at[f])

    def store_lin():
        return pltpu.make_async_copy(L.at[SUBSTEPS, :, pl.ds(8, ARC)], out_lin, outs.at[5])

    barrier = pltpu.get_barrier_semaphore()

    def greet(dev):
        pl.semaphore_signal(barrier, inc=1, device_id=dev, device_id_type=pl.DeviceIdType.MESH)

    for b in peers:
        greet((t, b))
    pl.when(not_last)(lambda: greet(right))
    pl.when(not_first)(lambda: greet(left))

    small = [
        pltpu.make_async_copy(src, dst, loc.at[7 + i])
        for i, (src, dst) in enumerate(
            ((fcn_in, fcn), (fcl_in, fcl), (fcy_in, fcy), (fcell_in, fcell), (frel_in, frel),
             (dif_in, dif), (yld_in, yld), (rat_in, rat))
        )
    ]
    for copy in small:
        copy.start()
    for f in ORDER:
        load_gas(f).start()
    load_lin().start()
    load_vel().start()

    zero_rows = jnp.zeros((8, SEG), F32)
    zero_band = jnp.zeros((BW, SEG), F32)

    def open_band(packed, dst):
        for h in range(CH):
            for wg in range(8):
                dst[h, 8 * wg:8 * wg + 8, :] = pltpu.roll(packed, 127 - 2 * (8 * wg + h), 1)

    def pack_band(s, f):
        acc = zero_rows
        for h in range(CH):
            for wg in range(8):
                idx = 8 * wg + h
                rows = S[s, f, h + 1, 8 + 8 * wg:16 + 8 * wg, :]
                acc = jnp.where(pair == idx, pltpu.roll(rows, 2 * idx + 1, 1), acc)
        GP[s, f] = acc

    def open_arc(packed, f):
        for i in range(LD):
            for g in range(4):
                EL[f * LD + i, 8 * g:8 * g + 8, :] = pltpu.roll(packed, 127 - 2 * (4 * i + g), 1)

    def pack_arc(s, f):
        acc = zero_rows
        for i in range(LD):
            for g in range(4):
                idx = 4 * i + g
                rows = L[s, f * LD + i, 8 + 8 * g:16 + 8 * g, :]
                acc = jnp.where(pair == idx, pltpu.roll(rows, 2 * idx + 1, 1), acc)
        LP[s, f] = acc

    def lining_margins(s):
        for b in range(NBLK):
            CD[s, b:b + 1, :] = L[s, b, 8:9, :]
            CU[s, b:b + 1, :] = L[s, b, 39:40, :]

    def own_surface(s):
        TL[s, arc_of(c), :] = L[s, 0, pl.ds(8, ARC), :]

    def own_walls(s):
        for h in range(CH):
            TGC[h:h + 1, :] = S[s, 0, h + 1, 8:9, :]
            TGC[CH + h:CH + h + 1, :] = S[s, 0, h + 1, 71:72, :]

        @pl.when(is_end)
        def _():
            TGC[16:ROWS, :] = S[s, 0, edge_row, mid, :]
            TGQ[s] = pick(CT[...], TGC[...])
            TGE[s, c // (NC - 1)] = TGQ[s, arc_of(c), :]

        @pl.when(jnp.logical_not(is_end))
        def _():
            for b in range(NC):
                TGP[s, 8 * b:8 * b + 8, :] = MSK[b, 0:8] * TGC[0:8, :] + MSK[b, 8:16] * TGC[8:16, :]
            TGM[s, eight_of(c), :] = TGP[s, eight_of(c), :]

    pl.semaphore_wait(
        barrier,
        NC - 1 + jnp.where(not_last, 1, 0) + jnp.where(not_first, 1, 0),
    )

    for f in ORDER:
        guarded(not_top, lambda: y_first(f, CH - 1, 0, up), "start")
        guarded(not_bottom, lambda: y_first(f, 0, 1, down), "start")
    for k in range(NC - 1):
        tl_first(k).start()
    for f in ORDER:
        load_gas(f).wait()
        pack_band(0, f)
        x_pair(0, f, "start")
    for copy in small:
        copy.wait()

    live = iota((1, ROWS), 1) < fcn[0]
    TB[c] = jnp.full((8, SEG), -1.0, F32)
    TB[c, 0:1, 0:ROWS] = jnp.where(live, fcl[...], -1).astype(F32)
    TB[c, 1:2, 0:ROWS] = jnp.where(live, fcy[...], -1).astype(F32)
    tb_group("start")
    load_lin().wait()
    lining_margins(0)
    c_pair(0, "start")
    for f in range(3):
        pack_arc(0, f)
    l_pair(0, "start")
    own_surface(0)

    def side_cell(r):
        return jnp.where(r < CH, r * BW, (r - CH) * BW + BW - 1)

    def edge_cell(h, w):
        return jnp.where((w > 0) & (w < BW - 1), h * BW + w, -2)

    slot = iota((ROWS, SEG), 0)
    own_cell = jnp.where(
        slot < 16,
        side_cell(slot),
        jnp.where(is_end, edge_cell(edge_row - 1, slot - 16), -2),
    ).astype(F32)
    rows_of = (own_cell == TB[c, 0:1, :]).astype(F32)
    cycle_of = (iota((256, SEG), 0).astype(F32) == TB[c, 1:2, :]).astype(BF16)
    seen_by = dot_nt(rows_of.astype(BF16), cycle_of)
    CM[...] = seen_by.astype(BF16)
    CT[...] = dot_nt(cycle_of, rows_of.astype(BF16)).astype(BF16)
    sides_seen = seen_by[0:16].astype(BF16)
    for b in range(NC):
        arc_rows = (iota((256, SEG), 0) // ARC == b).astype(BF16)
        MSK[b] = lax.dot_general(
            sides_seen, arc_rows, (((1,), (0,)), ((), ())), preferred_element_type=F32
        )
    NM[...] = jnp.broadcast_to(jnp.sum(rows_of, axis=1, keepdims=True), (ROWS, SEG))

    own_walls(0)
    tg_group(0, "start")


    @pl.loop(0, SUBSTEPS)
    def _(s):
        @pl.loop(0, NF)
        def _(f):
            @pl.loop(1, CH + 1)
            def _(h):
                S[s, f, h, 0:8, :] = zero_rows
                S[s, f, h, 72:80, :] = zero_rows

            @pl.when(c == 0)
            def _():
                S[s, f, 0, mid, :] = zero_band

            @pl.when(c == NC - 1)
            def _():
                S[s, f, CH + 1, mid, :] = zero_band

            @pl.when(t == 0)
            def _():
                GL[s, f] = zero_rows

            @pl.when(t == NT - 1)
            def _():
                GR[s, f] = zero_rows

        @pl.loop(0, 3)
        def _(f):
            @pl.when(t == 0)
            def _():
                LL[s, f] = zero_rows

            @pl.when(t == NT - 1)
            def _():
                LR[s, f] = zero_rows

        TGM[s, 0:8, :] = zero_rows
        TGM[s, 56:64, :] = zero_rows

    @pl.loop(0, CH)
    def _(h):
        WM[h] = zero_band

    cells = fcell[...]
    hw = cells // 4096 - c * (CH * BW)
    ax = cells % 4096 - t * SEG
    rel = frel[...]
    rel_a = rel.astype(BF16).astype(F32)
    rel_b = (rel - rel_a).astype(BF16).astype(F32)
    rel_c = rel - rel_a - rel_b
    axial_hot = iota((SEG, 256), 0) == ax
    weighted = jnp.concatenate(
        [jnp.where(axial_hot, part, 0.0).astype(BF16) for part in (rel_a, rel_b, rel_c)], axis=0
    )

    @pl.loop(0, CH)
    def _(h):
        hot = (iota((BW, 256), 0) + h * BW == hw).astype(BF16)
        total = dot_nt(hot, weighted)
        FS[h] = total[:, 0:SEG] + total[:, SEG:2 * SEG] + total[:, 2 * SEG:3 * SEG]

    load_vel().wait()

    burn = rat[0] * 2.0
    h_wall = rat[1] * 2.0
    gain_rate = rat[2] * h_wall
    evap = rat[6] * 4.0
    latent = rat[7] * 4.0

    def gas_slot(s, f):
        s1 = s + 1
        d = dif[f]
        react = yld[f] * burn * FIELD_SIGN[f]

        def band(h):
            q = S[s, f, h + 1, mid, :]
            ends = E[f, h]
            before = pltpu.roll(jnp.where(lane64 == SEG - 1, ends, q), 1, 1)
            after = pltpu.roll(jnp.where(lane64 == 0, ends, q), SEG - 1, 1)
            around = (
                S[s, f, h + 2, mid, :] + S[s, f, h, mid, :]
                + S[s, f, h + 1, 9:73, :] + S[s, f, h + 1, 7:71, :]
                + after + before
            )
            fuel = q if f == 2 else S[s, 2, h + 1, mid, :]
            new = q - V[h] * (q - before) + d * (around - 6.0 * q) + react * fuel
            if f == 2:
                new = new + FS[h]
            if f == 0:
                new = new - WM[h]
            S[s1, f, h + 1, mid, :] = new

        x_pair(s, f, "wait_recv")
        open_band(jnp.where(odd, GR[s, f], GL[s, f]), E.at[f])
        if INNER_FIRST:
            for h in range(1, CH - 1):
                band(h)
        y_pair(s, f, "wait_recv")
        band(0)
        band(CH - 1)

        @pl.when(s1 < SUBSTEPS)
        def _():
            y_pair(s1, f, "start")

        if not INNER_FIRST:
            for h in range(1, CH - 1):
                band(h)

        @pl.when(s1 < SUBSTEPS)
        def _():
            pack_band(s1, f)
            x_pair(s1, f, "start")

        @pl.when(s1 == SUBSTEPS)
        def _():
            store_gas(f).start()

    def wall_fluxes(s):
        tl_group(s, "wait_recv")
        for h in range(CH):
            TGC[h:h + 1, :] = S[s, 0, h + 1, 8:9, :]
            TGC[CH + h:CH + h + 1, :] = S[s, 0, h + 1, 71:72, :]

        def side_walls(seen):
            sides = h_wall * (NM[0:16, :] * TGC[0:16, :] - seen)
            for h in range(CH):
                WM[h, 0:1, :] = sides[h:h + 1]
                WM[h, BW - 1:BW, :] = sides[CH + h:CH + h + 1]

        @pl.when(is_end | (s == 0))
        def _():
            seen = pick(CM[...], TL[s])

            @pl.when(is_end)
            def _():
                WM[edge_row - 1] = h_wall * (NM[16:ROWS, :] * S[s, 0, edge_row, mid, :] - seen[16:ROWS])

            side_walls(seen[0:16])

        @pl.when(jnp.logical_not(is_end | (s == 0)))
        def _():
            seen = jnp.zeros((16, SEG), F32)
            for b in range(NC):
                rows = TLR[s, 8 * b:8 * b + 8, :]
                seen = seen + MSK[b] * jnp.concatenate([rows, rows], axis=0)
            side_walls(seen)

    def lining_tables():
        tb_group("wait_recv")
        r = iota((8 * NC, SEG), 0)
        k = (iota((ARC, SEG), 0) + c * ARC).astype(F32)

        def add(b, totals):
            heat, placed, count = totals
            here = r // 8 == b
            low = jnp.where(here, r % 8 * BW, -2).astype(F32)
            high = jnp.where(here, r % 8 * BW + BW - 1, -2).astype(F32)
            rows = ((low == TB[b, 0:1, :]) | (high == TB[b, 0:1, :])).astype(BF16)
            mine = (k == TB[b, 1:2, :]).astype(F32)
            hot = mine.astype(BF16)
            inner = (b > 0) & (b < NC - 1)
            heat = heat + jnp.where(inner, dot_nt(hot, rows), 0.0)
            placed = placed + dot_nt(rows, hot)
            return heat, placed, count + jnp.sum(mine, axis=1, keepdims=True)

        heat, placed, count = lax.fori_loop(
            0, NC, add,
            (jnp.zeros((ARC, 8 * NC), F32), jnp.zeros((8 * NC, ARC), F32), jnp.zeros((ARC, 1), F32)),
        )
        HM[...] = heat.astype(BF16)
        PT[...] = placed.astype(BF16)
        NK[...] = jnp.broadcast_to(count, (ARC, SEG))

    def lining_slot(s):
        s1 = s + 1
        pl.when(s == 0)(lining_tables)
        tg_group(s, "wait_recv")
        heat = pick(HM[...], TGM[s]) + TGE[s, 0] + TGE[s, 1]
        gain = gain_rate * (heat - NK[...] * L[s, 0, pl.ds(8, ARC), :])
        heat_now = L[s, 0:LD, pl.ds(8, ARC), :]
        soft = jnp.maximum(heat_now, 0.0) + jnp.log1p(jnp.exp(-jnp.abs(heat_now)))
        SE[...] = evap * L[s, LD:2 * LD, pl.ds(8, ARC), :] * soft
        l_pair(s, "wait_recv")
        for f in range(3):
            open_arc(jnp.where(odd, LR[s, f], LL[s, f]), f)
        c_pair(s, "wait_recv")
        for b in range(NBLK):
            L[s, b, 7:8, :] = HD[s, b:b + 1, :]
            L[s, b, 40:41, :] = HU[s, b:b + 1, :]

        def diffused(f, i):
            deep = min(i + 1, LD - 1)
            shallow = max(i - 1, 0)
            b = f * LD + i
            q = L[s, b, pl.ds(8, ARC), :]
            ends = EL[b]
            before = pltpu.roll(jnp.where(lane32 == SEG - 1, ends, q), 1, 1)
            after = pltpu.roll(jnp.where(lane32 == 0, ends, q), SEG - 1, 1)
            around = (
                L[s, f * LD + deep, pl.ds(8, ARC), :] + L[s, f * LD + shallow, pl.ds(8, ARC), :]
                + L[s, b, 9:41, :] + L[s, b, 7:39, :] + after + before
            )
            return q + rat[3 + f] * (around - 6.0 * q)

        L[s1, 0, pl.ds(8, ARC), :] = diffused(0, 0) - latent * SE[0] + gain

        @pl.when(s1 < SUBSTEPS)
        def _():
            own_surface(s1)
            TLP[s1] = pick(PT[...], L[s1, 0, pl.ds(8, ARC), :])
            TLR[s1, eight_of(c), :] = TLP[s1, eight_of(c), :]
            tl_group(s1, "start")

        for i in range(LD):
            e = SE[i]
            if i > 0:
                L[s1, i, pl.ds(8, ARC), :] = diffused(0, i) - latent * e
            L[s1, LD + i, pl.ds(8, ARC), :] = diffused(1, i) - e
            L[s1, 2 * LD + i, pl.ds(8, ARC), :] = diffused(2, i) + e

        @pl.when(s1 < SUBSTEPS)
        def _():
            lining_margins(s1)
            c_pair(s1, "start")
            for f in range(3):
                pack_arc(s1, f)
            l_pair(s1, "start")

        @pl.when(s1 == SUBSTEPS)
        def _():
            store_lin().start()

    @pl.loop(0, SUBSTEPS)
    def _(s):
        for f in ORDER[:4]:
            gas_slot(s, f)
        wall_fluxes(s)
        gas_slot(s, ORDER[4])

        @pl.when(s + 1 < SUBSTEPS)
        def _():
            own_walls(s + 1)
            tg_group(s + 1, "start")

        lining_slot(s)

    tb_group("wait_send")

    @pl.loop(0, SUBSTEPS)
    def _(s):
        for f in range(NF):
            x_pair(s, f, "wait_send")
            y_pair(s, f, "wait_send")
        l_pair(s, "wait_send")
        c_pair(s, "wait_send")
        tl_group(s, "wait_send")
        tg_group(s, "wait_send")

    for f in ORDER:
        store_gas(f).wait()
    store_lin().wait()


def on_device(gas, lining, velocity, diffusion, yields, rates, fire_cells, release, face_cells, face_cycle, face_count):
    lin = lining.reshape(NBLK, ARC, SEG)
    any_ = pl.BlockSpec(memory_space=pl.ANY)
    hbm = pl.BlockSpec(memory_space=pltpu.HBM)
    dma = pltpu.SemaphoreType.DMA
    n = SUBSTEPS
    out_gas, out_lin = pl.pallas_call(
        kernel,
        out_shape=(
            pltpu.VMEM((NF, CH, BW, SEG), F32),
            pltpu.VMEM((NBLK, ARC, SEG), F32),
        ),
        in_specs=[hbm] * 11,
        out_specs=(any_, any_),
        scratch_shapes=[
            pltpu.VMEM((n + 1, NF, CH + 2, 80, SEG), F32),
            pltpu.VMEM((n + 1, NBLK, 48, SEG), F32),
            pltpu.VMEM((CH, BW, SEG), F32),
            pltpu.VMEM((CH, BW, SEG), F32),
            pltpu.VMEM((CH, BW, SEG), F32),
            pltpu.VMEM((n, NF, 8, SEG), F32),
            pltpu.VMEM((n, NF, 8, SEG), F32),
            pltpu.VMEM((n, NF, 8, SEG), F32),
            pltpu.VMEM((n, 3, 8, SEG), F32),
            pltpu.VMEM((n, 3, 8, SEG), F32),
            pltpu.VMEM((n, 3, 8, SEG), F32),
            pltpu.VMEM((n, NBLK, SEG), F32),
            pltpu.VMEM((n, NBLK, SEG), F32),
            pltpu.VMEM((n, NBLK, SEG), F32),
            pltpu.VMEM((n, NBLK, SEG), F32),
            pltpu.VMEM((n, 256, SEG), F32),
            pltpu.VMEM((NC, 8, SEG), F32),
            pltpu.VMEM((ROWS, 256), BF16),
            pltpu.VMEM((256, ROWS), BF16),
            pltpu.VMEM((ROWS, SEG), F32),
            pltpu.VMEM((ARC, 8 * NC), BF16),
            pltpu.VMEM((8 * NC, ARC), BF16),
            pltpu.VMEM((ARC, SEG), F32),
            pltpu.VMEM((NC, 16, SEG), F32),
            pltpu.VMEM((n, 8 * NC, SEG), F32),
            pltpu.VMEM((n, 8 * NC, SEG), F32),
            pltpu.VMEM((ROWS, SEG), F32),
            pltpu.VMEM((n, 8 * NC, SEG), F32),
            pltpu.VMEM((n, 256, SEG), F32),
            pltpu.VMEM((n, 8 * NC, SEG), F32),
            pltpu.VMEM((n, 2, ARC, SEG), F32),
            pltpu.VMEM((NF, CH, BW, SEG), F32),
            pltpu.VMEM((NBLK, ARC, SEG), F32),
            pltpu.VMEM((LD, ARC, SEG), F32),
            pltpu.SMEM((NF,), F32),
            pltpu.SMEM((NF,), F32),
            pltpu.SMEM((8,), F32),
            pltpu.SMEM((1,), jnp.int32),
            pltpu.VMEM((1, 256), jnp.int32),
            pltpu.VMEM((1, 256), F32),
            pltpu.VMEM((1, ROWS), jnp.int32),
            pltpu.VMEM((1, ROWS), jnp.int32),
            dma((n, NF, 2)), dma((n, NF, 2)),
            dma((n, NF, 2)), dma((n, NF, 2)),
            dma((n, 2)), dma((n, 2)),
            dma((n, 2)), dma((n, 2)),
            dma((n, NC - 1)), dma((n, NC - 1)),
            dma((n, NC - 1)), dma((n, NC - 1)),
            dma((NC - 1,)), dma((NC - 1,)),
            dma((15,)), dma((6,)),
        ],
        compiler_params=pltpu.CompilerParams(
            collective_id=0, has_side_effects=True, vmem_limit_bytes=56 * 1024 * 1024
        ),
    )(
        gas, lin, velocity, diffusion, yields, rates,
        fire_cells.reshape(1, -1), release.reshape(1, -1),
        face_cells.reshape(1, -1), face_cycle.reshape(1, -1), face_count,
    )
    return out_gas, out_lin.reshape(lining.shape)


def solution(mesh):
    in_specs = (
        P(None, "cross", None, "tunnel"),
        P(None, None, "cross", "tunnel"),
        P("cross", None, "tunnel"),
        P(), P(), P(), P(), P(),
        P(("tunnel", "cross")),
        P(("tunnel", "cross")),
        P(("tunnel", "cross")),
    )
    out_specs = (P(None, "cross", None, "tunnel"), P(None, None, "cross", "tunnel"))
    return jax.shard_map(on_device, mesh=mesh, in_specs=in_specs, out_specs=out_specs, check_vma=False)
```

```python
import jax
import jax.numpy as jnp
from jax import lax
from jax.experimental import pallas as pl
from jax.experimental.pallas import tpu as pltpu
from jax.sharding import PartitionSpec as P

SUBSTEPS = 4
NF = 5
CH = 8
BW = 64
SEG = 128
LD = 16
ARC = 32
NBLK = 3 * LD
NT = 32
NC = 8
ROWS = 80
FIELD_SIGN = (1.0, 1.0, -1.0, 1.0, 1.0)
ORDER = (2, 1, 3, 4, 0)
F32 = jnp.float32
BF16 = jnp.bfloat16


def iota(shape, dim):
    return lax.broadcasted_iota(jnp.int32, shape, dim)


def dot_nt(a, b):
    return lax.dot_general(a, b, (((1,), (1,)), ((), ())), preferred_element_type=F32)


def pick(table, rows):
    a = rows.astype(BF16)
    rest = rows - a.astype(F32)
    b = rest.astype(BF16)
    d = (rest - b.astype(F32)).astype(BF16)
    parts = jnp.concatenate([a, b, d], axis=1)
    out = lax.dot_general(table, parts, (((1,), (0,)), ((), ())), preferred_element_type=F32)
    n = rows.shape[1]
    return out[:, 0:n] + out[:, n:2 * n] + out[:, 2 * n:3 * n]


def kernel(
    gas, lin, vel, dif_in, yld_in, rat_in, fcell_in, frel_in, fcl_in, fcy_in, fcn_in,
    out_gas, out_lin,
    S, L, V, FS, WM, GP, GL, GR, LP, LL, LR, CU, CD, HD, HU, TL, TB, CM, CT, NM, HM, PT, NK,
    MSK, TLP, TLR, TGC, TGP, TGQ, TGM, TGE, E, EL, SE, dif, yld, rat, fcn, fcell, frel, fcl, fcy,
    ys, yr, xs, xr, cs, cr, ls, lr, tls, tlr, tgs, tgr, tbs, tbr, loc,
):
    t = lax.axis_index("tunnel")
    c = lax.axis_index("cross")
    not_bottom = c > 0
    not_top = c < NC - 1
    not_first = t > 0
    not_last = t < NT - 1
    is_end = (c == 0) | (c == NC - 1)
    up = (t, (c + 1) % NC)
    down = (t, (c + NC - 1) % NC)
    right = (t + 1, c)
    left = (t - 1, c)
    peers = [(c + k) % NC for k in range(1, NC)]
    origins = [(c + NC - k) % NC for k in range(1, NC)]
    edge_row = jnp.where(c == NC - 1, CH, 1)
    lane = iota((8, SEG), 1)
    pair = lane // 2
    odd = lane % 2 == 1
    lane64 = iota((BW, SEG), 1)
    lane32 = iota((ARC, SEG), 1)

    def remote(src, dst, ssem, rsem, dev):
        return pltpu.make_async_remote_copy(
            src_ref=src, dst_ref=dst, send_sem=ssem, recv_sem=rsem,
            device_id=dev, device_id_type=pl.DeviceIdType.MESH,
        )

    mid = pl.ds(8, BW)

    def y_up(s, f):
        return remote(S.at[s, f, CH, mid], S.at[s, f, 0, mid], ys.at[s, f, 0], yr.at[s, f, 0], up)

    def y_down(s, f):
        return remote(S.at[s, f, 1, mid], S.at[s, f, CH + 1, mid], ys.at[s, f, 1], yr.at[s, f, 1], down)

    def y_first(f, row, side, dev):
        dst = S.at[0, f, (CH + 1) * side, mid]
        return remote(gas.at[f, row], dst, ys.at[0, f, side], yr.at[0, f, side], dev)

    def x_right(s, f):
        return remote(GP.at[s, f], GL.at[s, f], xs.at[s, f, 0], xr.at[s, f, 0], right)

    def x_left(s, f):
        return remote(GP.at[s, f], GR.at[s, f], xs.at[s, f, 1], xr.at[s, f, 1], left)

    def c_up(s):
        return remote(CU.at[s], HD.at[s], cs.at[s, 0], cr.at[s, 0], up)

    def c_down(s):
        return remote(CD.at[s], HU.at[s], cs.at[s, 1], cr.at[s, 1], down)

    def l_right(s):
        return remote(LP.at[s], LL.at[s], ls.at[s, 0], lr.at[s, 0], right)

    def l_left(s):
        return remote(LP.at[s], LR.at[s], ls.at[s, 1], lr.at[s, 1], left)

    def at_rim(b):
        return (b == 0) | (b == NC - 1)

    def arc_of(b):
        return pl.ds(pl.multiple_of(b * ARC, ARC), ARC)

    def eight_of(b):
        return pl.ds(pl.multiple_of(b * 8, 8), 8)

    def tl_whole(s, k):
        part = TL.at[s, arc_of(c)]
        return remote(part, part, tls.at[s, k], tlr.at[s, k], (t, peers[k]))

    def tl_first(k):
        return remote(lin.at[0], TL.at[0, arc_of(c)], tls.at[0, k], tlr.at[0, k], (t, peers[k]))

    def tl_placed(s, k):
        return remote(
            TLP.at[s, eight_of(peers[k])], TLR.at[s, eight_of(c)], tls.at[s, k], tlr.at[s, k], (t, peers[k])
        )

    def tg_mid(s, k):
        return remote(
            TGP.at[s, eight_of(peers[k])], TGM.at[s, eight_of(c)], tgs.at[s, k], tgr.at[s, k], (t, peers[k])
        )

    def tg_rim(s, k):
        return remote(
            TGQ.at[s, arc_of(peers[k])], TGE.at[s, c // (NC - 1)], tgs.at[s, k], tgr.at[s, k], (t, peers[k])
        )

    def tb_all(k):
        return remote(TB.at[c], TB.at[c], tbs.at[k], tbr.at[k], (t, peers[k]))

    def guarded(cond, copy, act):
        @pl.when(cond)
        def _():
            getattr(copy(), act)()

    def y_pair(s, f, act):
        guarded(not_top if act != "wait_recv" else not_bottom, lambda: y_up(s, f), act)
        guarded(not_bottom if act != "wait_recv" else not_top, lambda: y_down(s, f), act)

    def x_pair(s, f, act):
        guarded(not_last if act != "wait_recv" else not_first, lambda: x_right(s, f), act)
        guarded(not_first if act != "wait_recv" else not_last, lambda: x_left(s, f), act)

    def c_pair(s, act):
        getattr(c_up(s), act)()
        getattr(c_down(s), act)()

    def l_pair(s, act):
        guarded(not_last if act != "wait_recv" else not_first, lambda: l_right(s), act)
        guarded(not_first if act != "wait_recv" else not_last, lambda: l_left(s), act)

    def either(cond, one, two, act):
        guarded(cond, one, act)
        guarded(jnp.logical_not(cond), two, act)

    def tl_group(s, act):
        for k in range(NC - 1):
            whole = is_end if act == "wait_recv" else at_rim(peers[k])
            either(whole | (s == 0), lambda: tl_whole(s, k), lambda: tl_placed(s, k), act)

    def tg_group(s, act):
        for k in range(NC - 1):
            rim = at_rim(origins[k]) if act == "wait_recv" else is_end
            either(rim, lambda: tg_rim(s, k), lambda: tg_mid(s, k), act)

    def tb_group(act):
        for k in range(NC - 1):
            getattr(tb_all(k), act)()

    def load_gas(f):
        return pltpu.make_async_copy(gas.at[f], S.at[0, f, pl.ds(1, CH), mid], loc.at[f])

    def load_lin():
        return pltpu.make_async_copy(lin, L.at[0, :, pl.ds(8, ARC)], loc.at[5])

    def load_vel():
        return pltpu.make_async_copy(vel, V, loc.at[6])

    barrier = pltpu.get_barrier_semaphore()

    def greet(dev):
        pl.semaphore_signal(barrier, inc=1, device_id=dev, device_id_type=pl.DeviceIdType.MESH)

    for b in peers:
        greet((t, b))
    pl.when(not_last)(lambda: greet(right))
    pl.when(not_first)(lambda: greet(left))

    small = [
        pltpu.make_async_copy(src, dst, loc.at[7 + i])
        for i, (src, dst) in enumerate(
            ((fcn_in, fcn), (fcl_in, fcl), (fcy_in, fcy), (fcell_in, fcell), (frel_in, frel),
             (dif_in, dif), (yld_in, yld), (rat_in, rat))
        )
    ]
    for copy in small:
        copy.start()
    for f in ORDER:
        load_gas(f).start()
    load_lin().start()
    load_vel().start()

    zero_rows = jnp.zeros((8, SEG), F32)
    zero_band = jnp.zeros((BW, SEG), F32)

    def open_band(packed, dst):
        for h in range(CH):
            for wg in range(8):
                dst[h, 8 * wg:8 * wg + 8, :] = pltpu.roll(packed, 127 - 2 * (8 * wg + h), 1)

    def pack_band(s, f):
        acc = zero_rows
        for h in range(CH):
            for wg in range(8):
                idx = 8 * wg + h
                rows = S[s, f, h + 1, 8 + 8 * wg:16 + 8 * wg, :]
                acc = jnp.where(pair == idx, pltpu.roll(rows, 2 * idx + 1, 1), acc)
        GP[s, f] = acc

    def open_arc(packed, f):
        for i in range(LD):
            for g in range(4):
                EL[f * LD + i, 8 * g:8 * g + 8, :] = pltpu.roll(packed, 127 - 2 * (4 * i + g), 1)

    def pack_arc(s, f):
        acc = zero_rows
        for i in range(LD):
            for g in range(4):
                idx = 4 * i + g
                rows = L[s, f * LD + i, 8 + 8 * g:16 + 8 * g, :]
                acc = jnp.where(pair == idx, pltpu.roll(rows, 2 * idx + 1, 1), acc)
        LP[s, f] = acc

    def lining_margins(s):
        for b in range(NBLK):
            CD[s, b:b + 1, :] = L[s, b, 8:9, :]
            CU[s, b:b + 1, :] = L[s, b, 39:40, :]

    def own_surface(s):
        TL[s, arc_of(c), :] = L[s, 0, pl.ds(8, ARC), :]

    def own_walls(s):
        for h in range(CH):
            TGC[h:h + 1, :] = S[s, 0, h + 1, 8:9, :]
            TGC[CH + h:CH + h + 1, :] = S[s, 0, h + 1, 71:72, :]

        @pl.when(is_end)
        def _():
            TGC[16:ROWS, :] = S[s, 0, edge_row, mid, :]
            TGQ[s] = pick(CT[...], TGC[...])
            TGE[s, c // (NC - 1)] = TGQ[s, arc_of(c), :]

        @pl.when(jnp.logical_not(is_end))
        def _():
            for b in range(NC):
                TGP[s, 8 * b:8 * b + 8, :] = MSK[b, 0:8] * TGC[0:8, :] + MSK[b, 8:16] * TGC[8:16, :]
            TGM[s, eight_of(c), :] = TGP[s, eight_of(c), :]

    @pl.loop(0, SUBSTEPS)
    def _(s):
        @pl.loop(0, NF)
        def _(f):
            @pl.loop(1, CH + 1)
            def _(h):
                S[s, f, h, 0:8, :] = zero_rows
                S[s, f, h, 72:80, :] = zero_rows

            @pl.when(c == 0)
            def _():
                S[s, f, 0, mid, :] = zero_band

            @pl.when(c == NC - 1)
            def _():
                S[s, f, CH + 1, mid, :] = zero_band

            @pl.when(t == 0)
            def _():
                GL[s, f] = zero_rows

            @pl.when(t == NT - 1)
            def _():
                GR[s, f] = zero_rows

        @pl.loop(0, 3)
        def _(f):
            @pl.when(t == 0)
            def _():
                LL[s, f] = zero_rows

            @pl.when(t == NT - 1)
            def _():
                LR[s, f] = zero_rows

        TGM[s, 0:8, :] = zero_rows
        TGM[s, 56:64, :] = zero_rows

    @pl.loop(0, CH)
    def _(h):
        WM[h] = zero_band

    pl.semaphore_wait(
        barrier,
        NC - 1 + jnp.where(not_last, 1, 0) + jnp.where(not_first, 1, 0),
    )

    for f in ORDER:
        guarded(not_top, lambda: y_first(f, CH - 1, 0, up), "start")
        guarded(not_bottom, lambda: y_first(f, 0, 1, down), "start")
    for k in range(NC - 1):
        tl_first(k).start()
    for f in ORDER:
        load_gas(f).wait()
        pack_band(0, f)
        x_pair(0, f, "start")
    for copy in small:
        copy.wait()

    live = iota((1, ROWS), 1) < fcn[0]
    TB[c] = jnp.full((8, SEG), -1.0, F32)
    TB[c, 0:1, 0:ROWS] = jnp.where(live, fcl[...], -1).astype(F32)
    TB[c, 1:2, 0:ROWS] = jnp.where(live, fcy[...], -1).astype(F32)
    tb_group("start")
    def side_cell(r):
        return jnp.where(r < CH, r * BW, (r - CH) * BW + BW - 1)

    def edge_cell(h, w):
        return jnp.where((w > 0) & (w < BW - 1), h * BW + w, -2)

    slot = iota((ROWS, SEG), 0)
    own_cell = jnp.where(
        slot < 16,
        side_cell(slot),
        jnp.where(is_end, edge_cell(edge_row - 1, slot - 16), -2),
    ).astype(F32)
    rows_of = (own_cell == TB[c, 0:1, :]).astype(F32)
    cycle_of = (iota((256, SEG), 0).astype(F32) == TB[c, 1:2, :]).astype(BF16)
    seen_by = dot_nt(rows_of.astype(BF16), cycle_of)
    CM[...] = seen_by.astype(BF16)

    @pl.when(is_end)
    def _():
        CT[...] = dot_nt(cycle_of, rows_of.astype(BF16)).astype(BF16)

    seat = jnp.sum(rows_of[0:16] * TB[c, 1:2, :], axis=1, keepdims=True)
    taken = jnp.sum(rows_of[0:16], axis=1, keepdims=True) > 0.0
    for b in range(NC):
        here = taken & (seat >= b * ARC) & (seat < (b + 1) * ARC)
        MSK[b] = jnp.broadcast_to(here.astype(F32), (16, SEG))
    NM[...] = jnp.broadcast_to(jnp.sum(rows_of, axis=1, keepdims=True), (ROWS, SEG))

    own_walls(0)
    tg_group(0, "start")


    load_lin().wait()
    lining_margins(0)
    c_pair(0, "start")
    for f in range(3):
        pack_arc(0, f)
    l_pair(0, "start")
    own_surface(0)

    cells = fcell[...]
    hw = cells // 4096 - c * (CH * BW)
    ax = cells % 4096 - t * SEG
    rel = frel[...]
    rel_a = rel.astype(BF16).astype(F32)
    rel_b = (rel - rel_a).astype(BF16).astype(F32)
    rel_c = rel - rel_a - rel_b
    axial_hot = iota((SEG, 256), 0) == ax
    weighted = jnp.concatenate(
        [jnp.where(axial_hot, part, 0.0).astype(BF16) for part in (rel_a, rel_b, rel_c)], axis=0
    )

    @pl.loop(0, CH)
    def _(h):
        hot = (iota((BW, 256), 0) + h * BW == hw).astype(BF16)
        total = dot_nt(hot, weighted)
        FS[h] = total[:, 0:SEG] + total[:, SEG:2 * SEG] + total[:, 2 * SEG:3 * SEG]

    load_vel().wait()

    burn = rat[0] * 2.0
    h_wall = rat[1] * 2.0
    gain_rate = rat[2] * h_wall
    evap = rat[6] * 4.0
    latent = rat[7] * 4.0

    def gas_slot(s, f, after, last):
        s1 = s + 1
        d = dif[f]
        react = yld[f] * burn * FIELD_SIGN[f]

        def band(h):
            q = S[s, f, h + 1, mid, :]
            ends = E[f, h]
            before = pltpu.roll(jnp.where(lane64 == SEG - 1, ends, q), 1, 1)
            beyond = pltpu.roll(jnp.where(lane64 == 0, ends, q), SEG - 1, 1)
            around = (
                S[s, f, h + 2, mid, :] + S[s, f, h, mid, :]
                + S[s, f, h + 1, 9:73, :] + S[s, f, h + 1, 7:71, :]
                + beyond + before
            )
            fuel = q if f == 2 else S[s, 2, h + 1, mid, :]
            new = q - V[h] * (q - before) + d * (around - 6.0 * q) + react * fuel
            if f == 2:
                new = new + FS[h]
            if f == 0:
                new = new - WM[h]
            if last:
                out_gas[f, h] = new
            else:
                S[s1, f, h + 1, mid, :] = new

        y_pair(s, f, "wait_recv")
        band(0)
        band(CH - 1)
        if not last:
            y_pair(s1, f, "start")
        if after is not None:
            x_pair(s, after, "wait_recv")
            open_band(jnp.where(odd, GR[s, after], GL[s, after]), E.at[after])
        for h in range(1, CH - 1):
            band(h)
        if not last:
            pack_band(s1, f)
            x_pair(s1, f, "start")

    def wall_fluxes(s):
        tl_group(s, "wait_recv")
        for h in range(CH):
            TGC[h:h + 1, :] = S[s, 0, h + 1, 8:9, :]
            TGC[CH + h:CH + h + 1, :] = S[s, 0, h + 1, 71:72, :]

        def side_walls(seen):
            sides = h_wall * (NM[0:16, :] * TGC[0:16, :] - seen)
            for h in range(CH):
                WM[h, 0:1, :] = sides[h:h + 1]
                WM[h, BW - 1:BW, :] = sides[CH + h:CH + h + 1]

        @pl.when(is_end | (s == 0))
        def _():
            seen = pick(CM[...], TL[s])

            @pl.when(is_end)
            def _():
                WM[edge_row - 1] = h_wall * (NM[16:ROWS, :] * S[s, 0, edge_row, mid, :] - seen[16:ROWS])

            side_walls(seen[0:16])

        @pl.when(jnp.logical_not(is_end | (s == 0)))
        def _():
            seen = jnp.zeros((16, SEG), F32)
            for b in range(NC):
                rows = TLR[s, 8 * b:8 * b + 8, :]
                seen = seen + MSK[b] * jnp.concatenate([rows, rows], axis=0)
            side_walls(seen)

    def lining_tables():
        tb_group("wait_recv")
        r = iota((8 * NC, SEG), 0)
        k = (iota((ARC, SEG), 0) + c * ARC).astype(F32)

        def add(b, totals):
            heat, placed, count = totals
            here = r // 8 == b
            low = jnp.where(here, r % 8 * BW, -2).astype(F32)
            high = jnp.where(here, r % 8 * BW + BW - 1, -2).astype(F32)
            rows = ((low == TB[b, 0:1, :]) | (high == TB[b, 0:1, :])).astype(BF16)
            mine = (k == TB[b, 1:2, :]).astype(F32)
            hot = mine.astype(BF16)
            inner = (b > 0) & (b < NC - 1)
            heat = heat + jnp.where(inner, dot_nt(hot, rows), 0.0)
            placed = placed + dot_nt(rows, hot)
            return heat, placed, count + jnp.sum(mine, axis=1, keepdims=True)

        heat, placed, count = lax.fori_loop(
            0, NC, add,
            (jnp.zeros((ARC, 8 * NC), F32), jnp.zeros((8 * NC, ARC), F32), jnp.zeros((ARC, 1), F32)),
        )
        HM[...] = heat.astype(BF16)
        PT[...] = placed.astype(BF16)
        NK[...] = jnp.broadcast_to(count, (ARC, SEG))

    def lining_slot(s, last):
        s1 = s + 1
        if not last:
            pl.when(s == 0)(lining_tables)
        tg_group(s, "wait_recv")
        l_pair(s, "wait_recv")
        c_pair(s, "wait_recv")
        heat = pick(HM[...], TGM[s]) + TGE[s, 0] + TGE[s, 1]
        gain = gain_rate * (heat - NK[...] * L[s, 0, pl.ds(8, ARC), :])
        heat_now = L[s, 0:LD, pl.ds(8, ARC), :]
        soft = jnp.maximum(heat_now, 0.0) + jnp.log1p(jnp.exp(-jnp.abs(heat_now)))
        SE[...] = evap * L[s, LD:2 * LD, pl.ds(8, ARC), :] * soft
        for f in range(3):
            open_arc(jnp.where(odd, LR[s, f], LL[s, f]), f)
        for b in range(NBLK):
            L[s, b, 7:8, :] = HD[s, b:b + 1, :]
            L[s, b, 40:41, :] = HU[s, b:b + 1, :]

        def diffused(f, i):
            deep = min(i + 1, LD - 1)
            shallow = max(i - 1, 0)
            b = f * LD + i
            q = L[s, b, pl.ds(8, ARC), :]
            ends = EL[b]
            before = pltpu.roll(jnp.where(lane32 == SEG - 1, ends, q), 1, 1)
            after = pltpu.roll(jnp.where(lane32 == 0, ends, q), SEG - 1, 1)
            around = (
                L[s, f * LD + deep, pl.ds(8, ARC), :] + L[s, f * LD + shallow, pl.ds(8, ARC), :]
                + L[s, b, 9:41, :] + L[s, b, 7:39, :] + after + before
            )
            return q + rat[3 + f] * (around - 6.0 * q)

        def settle(b, value):
            if last:
                out_lin[b] = value
            else:
                L[s1, b, pl.ds(8, ARC), :] = value

        settle(0, diffused(0, 0) - latent * SE[0] + gain)
        if not last:
            own_surface(s1)
            TLP[s1] = pick(PT[...], L[s1, 0, pl.ds(8, ARC), :])
            TLR[s1, eight_of(c), :] = TLP[s1, eight_of(c), :]
            tl_group(s1, "start")

        for i in range(LD):
            e = SE[i]
            if i > 0:
                settle(i, diffused(0, i) - latent * e)
            settle(LD + i, diffused(1, i) - e)
            settle(2 * LD + i, diffused(2, i) + e)

        if not last:
            lining_margins(s1)
            for f in range(3):
                pack_arc(s1, f)
            c_pair(s1, "start")
            l_pair(s1, "start")

    def substep(s, last):
        first = ORDER[0]
        x_pair(s, first, "wait_recv")
        open_band(jnp.where(odd, GR[s, first], GL[s, first]), E.at[first])
        for f, after in zip(ORDER[:4], ORDER[1:]):
            gas_slot(s, f, after, last)
        wall_fluxes(s)
        gas_slot(s, ORDER[4], None, last)
        if not last:
            own_walls(s + 1)
            tg_group(s + 1, "start")
        lining_slot(s, last)

    @pl.loop(0, SUBSTEPS - 1)
    def _(s):
        substep(s, False)

    substep(SUBSTEPS - 1, True)

    tb_group("wait_send")

    @pl.loop(0, SUBSTEPS)
    def _(s):
        for f in range(NF):
            x_pair(s, f, "wait_send")
            y_pair(s, f, "wait_send")
        l_pair(s, "wait_send")
        c_pair(s, "wait_send")
        tl_group(s, "wait_send")
        tg_group(s, "wait_send")


def leave(gas, lin, shape):
    def body(gas_ref, lin_ref, out_gas, out_lin, sems):
        copies = [
            pltpu.make_async_copy(gas_ref, out_gas, sems.at[0]),
            pltpu.make_async_copy(lin_ref, out_lin, sems.at[1]),
        ]
        for copy in copies:
            copy.start()
        for copy in copies:
            copy.wait()

    out_gas, out_lin = pl.pallas_call(
        body,
        out_shape=(jax.ShapeDtypeStruct(gas.shape, F32), jax.ShapeDtypeStruct(lin.shape, F32)),
        in_specs=[pl.BlockSpec(memory_space=pl.ANY)] * 2,
        out_specs=(pl.BlockSpec(memory_space=pltpu.HBM),) * 2,
        scratch_shapes=[pltpu.SemaphoreType.DMA((2,))],
        compiler_params=pltpu.CompilerParams(vmem_limit_bytes=4 * 1024 * 1024),
    )(gas, lin)
    return out_gas, out_lin.reshape(shape)


def on_device(gas, lining, velocity, diffusion, yields, rates, fire_cells, release, face_cells, face_cycle, face_count):
    lin = lining.reshape(NBLK, ARC, SEG)
    any_ = pl.BlockSpec(memory_space=pl.ANY)
    hbm = pl.BlockSpec(memory_space=pltpu.HBM)
    dma = pltpu.SemaphoreType.DMA
    n = SUBSTEPS
    out_gas, out_lin = pl.pallas_call(
        kernel,
        out_shape=(
            pltpu.VMEM((NF, CH, BW, SEG), F32),
            pltpu.VMEM((NBLK, ARC, SEG), F32),
        ),
        in_specs=[hbm] * 11,
        out_specs=(pl.BlockSpec(memory_space=pltpu.VMEM),) * 2,
        scratch_shapes=[
            pltpu.VMEM((n, NF, CH + 2, 80, SEG), F32),
            pltpu.VMEM((n, NBLK, 48, SEG), F32),
            pltpu.VMEM((CH, BW, SEG), F32),
            pltpu.VMEM((CH, BW, SEG), F32),
            pltpu.VMEM((CH, BW, SEG), F32),
            pltpu.VMEM((n, NF, 8, SEG), F32),
            pltpu.VMEM((n, NF, 8, SEG), F32),
            pltpu.VMEM((n, NF, 8, SEG), F32),
            pltpu.VMEM((n, 3, 8, SEG), F32),
            pltpu.VMEM((n, 3, 8, SEG), F32),
            pltpu.VMEM((n, 3, 8, SEG), F32),
            pltpu.VMEM((n, NBLK, SEG), F32),
            pltpu.VMEM((n, NBLK, SEG), F32),
            pltpu.VMEM((n, NBLK, SEG), F32),
            pltpu.VMEM((n, NBLK, SEG), F32),
            pltpu.VMEM((n, 256, SEG), F32),
            pltpu.VMEM((NC, 8, SEG), F32),
            pltpu.VMEM((ROWS, 256), BF16),
            pltpu.VMEM((256, ROWS), BF16),
            pltpu.VMEM((ROWS, SEG), F32),
            pltpu.VMEM((ARC, 8 * NC), BF16),
            pltpu.VMEM((8 * NC, ARC), BF16),
            pltpu.VMEM((ARC, SEG), F32),
            pltpu.VMEM((NC, 16, SEG), F32),
            pltpu.VMEM((n, 8 * NC, SEG), F32),
            pltpu.VMEM((n, 8 * NC, SEG), F32),
            pltpu.VMEM((ROWS, SEG), F32),
            pltpu.VMEM((n, 8 * NC, SEG), F32),
            pltpu.VMEM((n, 256, SEG), F32),
            pltpu.VMEM((n, 8 * NC, SEG), F32),
            pltpu.VMEM((n, 2, ARC, SEG), F32),
            pltpu.VMEM((NF, CH, BW, SEG), F32),
            pltpu.VMEM((NBLK, ARC, SEG), F32),
            pltpu.VMEM((LD, ARC, SEG), F32),
            pltpu.SMEM((NF,), F32),
            pltpu.SMEM((NF,), F32),
            pltpu.SMEM((8,), F32),
            pltpu.SMEM((1,), jnp.int32),
            pltpu.VMEM((1, 256), jnp.int32),
            pltpu.VMEM((1, 256), F32),
            pltpu.VMEM((1, ROWS), jnp.int32),
            pltpu.VMEM((1, ROWS), jnp.int32),
            dma((n, NF, 2)), dma((n, NF, 2)),
            dma((n, NF, 2)), dma((n, NF, 2)),
            dma((n, 2)), dma((n, 2)),
            dma((n, 2)), dma((n, 2)),
            dma((n, NC - 1)), dma((n, NC - 1)),
            dma((n, NC - 1)), dma((n, NC - 1)),
            dma((NC - 1,)), dma((NC - 1,)),
            dma((15,)),
        ],
        compiler_params=pltpu.CompilerParams(
            collective_id=0, has_side_effects=True, vmem_limit_bytes=56 * 1024 * 1024
        ),
    )(
        gas, lin, velocity, diffusion, yields, rates,
        fire_cells.reshape(1, -1), release.reshape(1, -1),
        face_cells.reshape(1, -1), face_cycle.reshape(1, -1), face_count,
    )
    return leave(out_gas, out_lin, lining.shape)


def solution(mesh):
    in_specs = (
        P(None, "cross", None, "tunnel"),
        P(None, None, "cross", "tunnel"),
        P("cross", None, "tunnel"),
        P(), P(), P(), P(), P(),
        P(("tunnel", "cross")),
        P(("tunnel", "cross")),
        P(("tunnel", "cross")),
    )
    out_specs = (P(None, "cross", None, "tunnel"), P(None, None, "cross", "tunnel"))
    return jax.shard_map(on_device, mesh=mesh, in_specs=in_specs, out_specs=out_specs, check_vma=False)
```

```python
import jax
import jax.numpy as jnp
from jax import lax
from jax.experimental import pallas as pl
from jax.experimental.pallas import tpu as pltpu
from jax.sharding import PartitionSpec as P

SUBSTEPS = 4
NF = 5
CH = 8
BW = 64
SEG = 128
LD = 16
ARC = 32
NBLK = 3 * LD
NT = 32
NC = 8
ROWS = 80
FIELD_SIGN = (1.0, 1.0, -1.0, 1.0, 1.0)
ORDER = (2, 1, 3, 4, 0)
F32 = jnp.float32
BF16 = jnp.bfloat16


def iota(shape, dim):
    return lax.broadcasted_iota(jnp.int32, shape, dim)


def dot_nt(a, b):
    return lax.dot_general(a, b, (((1,), (1,)), ((), ())), preferred_element_type=F32)


def pick(table, rows):
    a = rows.astype(BF16)
    rest = rows - a.astype(F32)
    b = rest.astype(BF16)
    d = (rest - b.astype(F32)).astype(BF16)
    parts = jnp.concatenate([a, b, d], axis=1)
    out = lax.dot_general(table, parts, (((1,), (0,)), ((), ())), preferred_element_type=F32)
    n = rows.shape[1]
    return out[:, 0:n] + out[:, n:2 * n] + out[:, 2 * n:3 * n]


def kernel(
    gas, lin, vel, dif_in, yld_in, rat_in, fcell_in, frel_in, fcl_in, fcy_in, fcn_in,
    out_gas, out_lin,
    S, L, V, FS, WM, GP, GL, GR, LP, LL, LR, CU, CD, HD, HU, TL, TB, CM, CT, NM, HM, PT, NK,
    MSK, TLP, TLR, TGC, TGP, TGQ, TGM, TGE, E, EL, SE, dif, yld, rat, fcn, fcell, frel, fcl, fcy,
    ys, yr, xs, xr, cs, cr, ls, lr, tls, tlr, tgs, tgr, tbs, tbr, loc,
):
    t = lax.axis_index("tunnel")
    c = lax.axis_index("cross")
    not_bottom = c > 0
    not_top = c < NC - 1
    not_first = t > 0
    not_last = t < NT - 1
    is_end = (c == 0) | (c == NC - 1)
    up = (t, (c + 1) % NC)
    down = (t, (c + NC - 1) % NC)
    right = (t + 1, c)
    left = (t - 1, c)
    peers = [(c + k) % NC for k in range(1, NC)]
    origins = [(c + NC - k) % NC for k in range(1, NC)]
    edge_row = jnp.where(c == NC - 1, CH, 1)
    lane = iota((8, SEG), 1)
    pair = lane // 2
    odd = lane % 2 == 1
    lane64 = iota((BW, SEG), 1)
    lane32 = iota((ARC, SEG), 1)

    def remote(src, dst, ssem, rsem, dev):
        return pltpu.make_async_remote_copy(
            src_ref=src, dst_ref=dst, send_sem=ssem, recv_sem=rsem,
            device_id=dev, device_id_type=pl.DeviceIdType.MESH,
        )

    mid = pl.ds(8, BW)

    def y_up(s, f):
        return remote(S.at[s, f, CH, mid], S.at[s, f, 0, mid], ys.at[s, f, 0], yr.at[s, f, 0], up)

    def y_down(s, f):
        return remote(S.at[s, f, 1, mid], S.at[s, f, CH + 1, mid], ys.at[s, f, 1], yr.at[s, f, 1], down)

    def y_first(f, row, side, dev):
        dst = S.at[0, f, (CH + 1) * side, mid]
        return remote(gas.at[f, row], dst, ys.at[0, f, side], yr.at[0, f, side], dev)

    def x_right(s, f):
        return remote(GP.at[s, f], GL.at[s, f], xs.at[s, f, 0], xr.at[s, f, 0], right)

    def x_left(s, f):
        return remote(GP.at[s, f], GR.at[s, f], xs.at[s, f, 1], xr.at[s, f, 1], left)

    def c_up(s):
        return remote(CU.at[s], HD.at[s], cs.at[s, 0], cr.at[s, 0], up)

    def c_down(s):
        return remote(CD.at[s], HU.at[s], cs.at[s, 1], cr.at[s, 1], down)

    def l_right(s):
        return remote(LP.at[s], LL.at[s], ls.at[s, 0], lr.at[s, 0], right)

    def l_left(s):
        return remote(LP.at[s], LR.at[s], ls.at[s, 1], lr.at[s, 1], left)

    def at_rim(b):
        return (b == 0) | (b == NC - 1)

    def arc_of(b):
        return pl.ds(pl.multiple_of(b * ARC, ARC), ARC)

    def eight_of(b):
        return pl.ds(pl.multiple_of(b * 8, 8), 8)

    def tl_whole(s, k):
        part = TL.at[s, arc_of(c)]
        return remote(part, part, tls.at[s, k], tlr.at[s, k], (t, peers[k]))

    def tl_first(k):
        return remote(lin.at[0], TL.at[0, arc_of(c)], tls.at[0, k], tlr.at[0, k], (t, peers[k]))

    def tl_placed(s, k):
        return remote(
            TLP.at[s, eight_of(peers[k])], TLR.at[s, eight_of(c)], tls.at[s, k], tlr.at[s, k], (t, peers[k])
        )

    def tg_mid(s, k):
        return remote(
            TGP.at[s, eight_of(peers[k])], TGM.at[s, eight_of(c)], tgs.at[s, k], tgr.at[s, k], (t, peers[k])
        )

    def tg_rim(s, k):
        return remote(
            TGQ.at[s, arc_of(peers[k])], TGE.at[s, c // (NC - 1)], tgs.at[s, k], tgr.at[s, k], (t, peers[k])
        )

    def tb_all(k):
        return remote(TB.at[c], TB.at[c], tbs.at[k], tbr.at[k], (t, peers[k]))

    def guarded(cond, copy, act):
        @pl.when(cond)
        def _():
            getattr(copy(), act)()

    def y_pair(s, f, act):
        guarded(not_top if act != "wait_recv" else not_bottom, lambda: y_up(s, f), act)
        guarded(not_bottom if act != "wait_recv" else not_top, lambda: y_down(s, f), act)

    def x_pair(s, f, act):
        guarded(not_last if act != "wait_recv" else not_first, lambda: x_right(s, f), act)
        guarded(not_first if act != "wait_recv" else not_last, lambda: x_left(s, f), act)

    def c_pair(s, act):
        getattr(c_up(s), act)()
        getattr(c_down(s), act)()

    def l_pair(s, act):
        guarded(not_last if act != "wait_recv" else not_first, lambda: l_right(s), act)
        guarded(not_first if act != "wait_recv" else not_last, lambda: l_left(s), act)

    def either(cond, one, two, act):
        guarded(cond, one, act)
        guarded(jnp.logical_not(cond), two, act)

    def tl_group(s, act):
        for k in range(NC - 1):
            whole = is_end if act == "wait_recv" else at_rim(peers[k])
            either(whole | (s == 0), lambda: tl_whole(s, k), lambda: tl_placed(s, k), act)

    def tg_group(s, act):
        for k in range(NC - 1):
            rim = at_rim(origins[k]) if act == "wait_recv" else is_end
            either(rim, lambda: tg_rim(s, k), lambda: tg_mid(s, k), act)

    def tb_group(act):
        for k in range(NC - 1):
            getattr(tb_all(k), act)()

    def load_gas(f):
        return pltpu.make_async_copy(gas.at[f], S.at[0, f, pl.ds(1, CH), mid], loc.at[f])

    def load_lin():
        return pltpu.make_async_copy(lin, L.at[0, :, pl.ds(8, ARC)], loc.at[5])

    def load_vel():
        return pltpu.make_async_copy(vel, V, loc.at[6])

    barrier = pltpu.get_barrier_semaphore()

    def greet(dev):
        pl.semaphore_signal(barrier, inc=1, device_id=dev, device_id_type=pl.DeviceIdType.MESH)

    for b in peers:
        greet((t, b))
    pl.when(not_last)(lambda: greet(right))
    pl.when(not_first)(lambda: greet(left))

    small = [
        pltpu.make_async_copy(src, dst, loc.at[7 + i])
        for i, (src, dst) in enumerate(
            ((fcn_in, fcn), (fcl_in, fcl), (fcy_in, fcy), (fcell_in, fcell), (frel_in, frel),
             (dif_in, dif), (yld_in, yld), (rat_in, rat))
        )
    ]
    for copy in small:
        copy.start()
    for f in ORDER:
        load_gas(f).start()
    load_lin().start()
    load_vel().start()

    zero_rows = jnp.zeros((8, SEG), F32)
    zero_band = jnp.zeros((BW, SEG), F32)

    def open_band(packed, dst):
        for h in range(CH):
            for wg in range(8):
                dst[h, 8 * wg:8 * wg + 8, :] = pltpu.roll(packed, 127 - 2 * (8 * wg + h), 1)

    def pack_band(s, f):
        acc = zero_rows
        for h in range(CH):
            for wg in range(8):
                idx = 8 * wg + h
                rows = S[s, f, h + 1, 8 + 8 * wg:16 + 8 * wg, :]
                acc = jnp.where(pair == idx, pltpu.roll(rows, 2 * idx + 1, 1), acc)
        GP[s, f] = acc

    def open_arc(packed, f):
        for i in range(LD):
            for g in range(4):
                EL[f * LD + i, 8 * g:8 * g + 8, :] = pltpu.roll(packed, 127 - 2 * (4 * i + g), 1)

    def pack_arc(s, f):
        acc = zero_rows
        for i in range(LD):
            for g in range(4):
                idx = 4 * i + g
                rows = L[s, f * LD + i, 8 + 8 * g:16 + 8 * g, :]
                acc = jnp.where(pair == idx, pltpu.roll(rows, 2 * idx + 1, 1), acc)
        LP[s, f] = acc

    def lining_margins(s):
        for b in range(NBLK):
            CD[s, b:b + 1, :] = L[s, b, 8:9, :]
            CU[s, b:b + 1, :] = L[s, b, 39:40, :]

    def own_surface(s):
        TL[s, arc_of(c), :] = L[s, 0, pl.ds(8, ARC), :]

    def own_walls(s):
        for h in range(CH):
            TGC[h:h + 1, :] = S[s, 0, h + 1, 8:9, :]
            TGC[CH + h:CH + h + 1, :] = S[s, 0, h + 1, 71:72, :]

        @pl.when(is_end)
        def _():
            TGC[16:ROWS, :] = S[s, 0, edge_row, mid, :]
            TGQ[s] = pick(CT[...], TGC[...])
            TGE[s, c // (NC - 1)] = TGQ[s, arc_of(c), :]

        @pl.when(jnp.logical_not(is_end))
        def _():
            for b in range(NC):
                TGP[s, 8 * b:8 * b + 8, :] = MSK[b, 0:8] * TGC[0:8, :] + MSK[b, 8:16] * TGC[8:16, :]
            TGM[s, eight_of(c), :] = TGP[s, eight_of(c), :]

    @pl.loop(0, SUBSTEPS)
    def _(s):
        @pl.loop(0, NF)
        def _(f):
            @pl.loop(1, CH + 1)
            def _(h):
                S[s, f, h, 0:8, :] = zero_rows
                S[s, f, h, 72:80, :] = zero_rows

            @pl.when(c == 0)
            def _():
                S[s, f, 0, mid, :] = zero_band

            @pl.when(c == NC - 1)
            def _():
                S[s, f, CH + 1, mid, :] = zero_band

            @pl.when(t == 0)
            def _():
                GL[s, f] = zero_rows

            @pl.when(t == NT - 1)
            def _():
                GR[s, f] = zero_rows

        @pl.loop(0, 3)
        def _(f):
            @pl.when(t == 0)
            def _():
                LL[s, f] = zero_rows

            @pl.when(t == NT - 1)
            def _():
                LR[s, f] = zero_rows

        TGM[s, 0:8, :] = zero_rows
        TGM[s, 56:64, :] = zero_rows

    @pl.loop(0, CH)
    def _(h):
        WM[h] = zero_band

    pl.semaphore_wait(
        barrier,
        NC - 1 + jnp.where(not_last, 1, 0) + jnp.where(not_first, 1, 0),
    )

    for f in ORDER:
        guarded(not_top, lambda: y_first(f, CH - 1, 0, up), "start")
        guarded(not_bottom, lambda: y_first(f, 0, 1, down), "start")
    for k in range(NC - 1):
        tl_first(k).start()
    for f in ORDER:
        load_gas(f).wait()
        pack_band(0, f)
        x_pair(0, f, "start")
    for copy in small:
        copy.wait()

    live = iota((1, ROWS), 1) < fcn[0]
    TB[c] = jnp.full((8, SEG), -1.0, F32)
    TB[c, 0:1, 0:ROWS] = jnp.where(live, fcl[...], -1).astype(F32)
    TB[c, 1:2, 0:ROWS] = jnp.where(live, fcy[...], -1).astype(F32)
    tb_group("start")
    def side_cell(r):
        return jnp.where(r < CH, r * BW, (r - CH) * BW + BW - 1)

    def edge_cell(h, w):
        return jnp.where((w > 0) & (w < BW - 1), h * BW + w, -2)

    slot = iota((ROWS, SEG), 0)
    own_cell = jnp.where(
        slot < 16,
        side_cell(slot),
        jnp.where(is_end, edge_cell(edge_row - 1, slot - 16), -2),
    ).astype(F32)
    rows_of = (own_cell == TB[c, 0:1, :]).astype(F32)
    cycle_of = (iota((256, SEG), 0).astype(F32) == TB[c, 1:2, :]).astype(BF16)
    seen_by = dot_nt(rows_of.astype(BF16), cycle_of)
    CM[...] = seen_by.astype(BF16)

    @pl.when(is_end)
    def _():
        CT[...] = dot_nt(cycle_of, rows_of.astype(BF16)).astype(BF16)

    seat = jnp.sum(rows_of[0:16] * TB[c, 1:2, :], axis=1, keepdims=True)
    taken = jnp.sum(rows_of[0:16], axis=1, keepdims=True) > 0.0
    for b in range(NC):
        here = taken & (seat >= b * ARC) & (seat < (b + 1) * ARC)
        MSK[b] = jnp.broadcast_to(here.astype(F32), (16, SEG))
    NM[...] = jnp.broadcast_to(jnp.sum(rows_of, axis=1, keepdims=True), (ROWS, SEG))

    own_walls(0)
    tg_group(0, "start")


    load_lin().wait()
    lining_margins(0)
    c_pair(0, "start")
    for f in range(3):
        pack_arc(0, f)
    l_pair(0, "start")
    own_surface(0)

    cells = fcell[...]
    hw = cells // 4096 - c * (CH * BW)
    ax = cells % 4096 - t * SEG
    rel = frel[...]
    rel_a = rel.astype(BF16).astype(F32)
    rel_b = (rel - rel_a).astype(BF16).astype(F32)
    rel_c = rel - rel_a - rel_b
    axial_hot = iota((SEG, 256), 0) == ax
    weighted = jnp.concatenate(
        [jnp.where(axial_hot, part, 0.0).astype(BF16) for part in (rel_a, rel_b, rel_c)], axis=0
    )

    @pl.loop(0, CH)
    def _(h):
        hot = (iota((BW, 256), 0) + h * BW == hw).astype(BF16)
        total = dot_nt(hot, weighted)
        FS[h] = total[:, 0:SEG] + total[:, SEG:2 * SEG] + total[:, 2 * SEG:3 * SEG]

    load_vel().wait()

    burn = rat[0] * 2.0
    h_wall = rat[1] * 2.0
    gain_rate = rat[2] * h_wall
    evap = rat[6] * 4.0
    latent = rat[7] * 4.0

    def gas_slot(s, f, after, last):
        s1 = s + 1
        d = dif[f]
        react = yld[f] * burn * FIELD_SIGN[f]

        def band(h):
            q = S[s, f, h + 1, mid, :]
            ends = E[f, h]
            before = pltpu.roll(jnp.where(lane64 == SEG - 1, ends, q), 1, 1)
            beyond = pltpu.roll(jnp.where(lane64 == 0, ends, q), SEG - 1, 1)
            around = (
                S[s, f, h + 2, mid, :] + S[s, f, h, mid, :]
                + S[s, f, h + 1, 9:73, :] + S[s, f, h + 1, 7:71, :]
                + beyond + before
            )
            fuel = q if f == 2 else S[s, 2, h + 1, mid, :]
            new = q - V[h] * (q - before) + d * (around - 6.0 * q) + react * fuel
            if f == 2:
                new = new + FS[h]
            if f == 0:
                new = new - WM[h]
            if last:
                out_gas[f, h] = new
            else:
                S[s1, f, h + 1, mid, :] = new

        if after is not None:
            x_pair(s, after, "wait_recv")
            open_band(jnp.where(odd, GR[s, after], GL[s, after]), E.at[after])
        for h in range(1, CH - 1):
            band(h)
        y_pair(s, f, "wait_recv")
        band(0)
        band(CH - 1)
        if not last:
            y_pair(s1, f, "start")
            pack_band(s1, f)
            x_pair(s1, f, "start")

    def wall_fluxes(s):
        tl_group(s, "wait_recv")
        for h in range(CH):
            TGC[h:h + 1, :] = S[s, 0, h + 1, 8:9, :]
            TGC[CH + h:CH + h + 1, :] = S[s, 0, h + 1, 71:72, :]

        def side_walls(seen):
            sides = h_wall * (NM[0:16, :] * TGC[0:16, :] - seen)
            for h in range(CH):
                WM[h, 0:1, :] = sides[h:h + 1]
                WM[h, BW - 1:BW, :] = sides[CH + h:CH + h + 1]

        @pl.when(is_end | (s == 0))
        def _():
            seen = pick(CM[...], TL[s])

            @pl.when(is_end)
            def _():
                WM[edge_row - 1] = h_wall * (NM[16:ROWS, :] * S[s, 0, edge_row, mid, :] - seen[16:ROWS])

            side_walls(seen[0:16])

        @pl.when(jnp.logical_not(is_end | (s == 0)))
        def _():
            seen = jnp.zeros((16, SEG), F32)
            for b in range(NC):
                rows = TLR[s, 8 * b:8 * b + 8, :]
                seen = seen + MSK[b] * jnp.concatenate([rows, rows], axis=0)
            side_walls(seen)

    def lining_tables():
        tb_group("wait_recv")
        r = iota((8 * NC, SEG), 0)
        k = (iota((ARC, SEG), 0) + c * ARC).astype(F32)

        def add(b, totals):
            heat, placed, count = totals
            here = r // 8 == b
            low = jnp.where(here, r % 8 * BW, -2).astype(F32)
            high = jnp.where(here, r % 8 * BW + BW - 1, -2).astype(F32)
            rows = ((low == TB[b, 0:1, :]) | (high == TB[b, 0:1, :])).astype(BF16)
            mine = (k == TB[b, 1:2, :]).astype(F32)
            hot = mine.astype(BF16)
            inner = (b > 0) & (b < NC - 1)
            heat = heat + jnp.where(inner, dot_nt(hot, rows), 0.0)
            placed = placed + dot_nt(rows, hot)
            return heat, placed, count + jnp.sum(mine, axis=1, keepdims=True)

        heat, placed, count = lax.fori_loop(
            0, NC, add,
            (jnp.zeros((ARC, 8 * NC), F32), jnp.zeros((8 * NC, ARC), F32), jnp.zeros((ARC, 1), F32)),
        )
        HM[...] = heat.astype(BF16)
        PT[...] = placed.astype(BF16)
        NK[...] = jnp.broadcast_to(count, (ARC, SEG))

    def lining_slot(s, last):
        s1 = s + 1
        if not last:
            pl.when(s == 0)(lining_tables)
        tg_group(s, "wait_recv")
        l_pair(s, "wait_recv")
        c_pair(s, "wait_recv")
        heat = pick(HM[...], TGM[s]) + TGE[s, 0] + TGE[s, 1]
        gain = gain_rate * (heat - NK[...] * L[s, 0, pl.ds(8, ARC), :])
        heat_now = L[s, 0:LD, pl.ds(8, ARC), :]
        soft = jnp.maximum(heat_now, 0.0) + jnp.log1p(jnp.exp(-jnp.abs(heat_now)))
        SE[...] = evap * L[s, LD:2 * LD, pl.ds(8, ARC), :] * soft
        for f in range(3):
            open_arc(jnp.where(odd, LR[s, f], LL[s, f]), f)
        for b in range(NBLK):
            L[s, b, 7:8, :] = HD[s, b:b + 1, :]
            L[s, b, 40:41, :] = HU[s, b:b + 1, :]

        def diffused(f, i):
            deep = min(i + 1, LD - 1)
            shallow = max(i - 1, 0)
            b = f * LD + i
            q = L[s, b, pl.ds(8, ARC), :]
            ends = EL[b]
            before = pltpu.roll(jnp.where(lane32 == SEG - 1, ends, q), 1, 1)
            after = pltpu.roll(jnp.where(lane32 == 0, ends, q), SEG - 1, 1)
            around = (
                L[s, f * LD + deep, pl.ds(8, ARC), :] + L[s, f * LD + shallow, pl.ds(8, ARC), :]
                + L[s, b, 9:41, :] + L[s, b, 7:39, :] + after + before
            )
            return q + rat[3 + f] * (around - 6.0 * q)

        def settle(b, value):
            if last:
                out_lin[b] = value
            else:
                L[s1, b, pl.ds(8, ARC), :] = value

        settle(0, diffused(0, 0) - latent * SE[0] + gain)
        if not last:
            own_surface(s1)
            TLP[s1] = pick(PT[...], L[s1, 0, pl.ds(8, ARC), :])
            TLR[s1, eight_of(c), :] = TLP[s1, eight_of(c), :]
            tl_group(s1, "start")
            tg_group(s1, "start")

        for i in range(LD):
            e = SE[i]
            if i > 0:
                settle(i, diffused(0, i) - latent * e)
            settle(LD + i, diffused(1, i) - e)
            settle(2 * LD + i, diffused(2, i) + e)

        if not last:
            lining_margins(s1)
            for f in range(3):
                pack_arc(s1, f)
            c_pair(s1, "start")
            l_pair(s1, "start")

    def substep(s, last):
        first = ORDER[0]
        x_pair(s, first, "wait_recv")
        open_band(jnp.where(odd, GR[s, first], GL[s, first]), E.at[first])
        for f, after in zip(ORDER[:4], ORDER[1:]):
            gas_slot(s, f, after, last)
        wall_fluxes(s)
        gas_slot(s, ORDER[4], None, last)
        if not last:
            own_walls(s + 1)
        lining_slot(s, last)

    @pl.loop(0, SUBSTEPS - 1)
    def _(s):
        substep(s, False)

    substep(SUBSTEPS - 1, True)

    tb_group("wait_send")

    @pl.loop(0, SUBSTEPS)
    def _(s):
        for f in range(NF):
            x_pair(s, f, "wait_send")
            y_pair(s, f, "wait_send")
        l_pair(s, "wait_send")
        c_pair(s, "wait_send")
        tl_group(s, "wait_send")
        tg_group(s, "wait_send")


def leave(gas, lin, shape):
    def body(gas_ref, lin_ref, out_gas, out_lin, sems):
        copies = [
            pltpu.make_async_copy(gas_ref, out_gas, sems.at[0]),
            pltpu.make_async_copy(lin_ref, out_lin, sems.at[1]),
        ]
        for copy in copies:
            copy.start()
        for copy in copies:
            copy.wait()

    out_gas, out_lin = pl.pallas_call(
        body,
        out_shape=(jax.ShapeDtypeStruct(gas.shape, F32), jax.ShapeDtypeStruct(lin.shape, F32)),
        in_specs=[pl.BlockSpec(memory_space=pl.ANY)] * 2,
        out_specs=(pl.BlockSpec(memory_space=pltpu.HBM),) * 2,
        scratch_shapes=[pltpu.SemaphoreType.DMA((2,))],
        compiler_params=pltpu.CompilerParams(vmem_limit_bytes=4 * 1024 * 1024),
    )(gas, lin)
    return out_gas, out_lin.reshape(shape)


def on_device(gas, lining, velocity, diffusion, yields, rates, fire_cells, release, face_cells, face_cycle, face_count):
    lin = lining.reshape(NBLK, ARC, SEG)
    any_ = pl.BlockSpec(memory_space=pl.ANY)
    hbm = pl.BlockSpec(memory_space=pltpu.HBM)
    dma = pltpu.SemaphoreType.DMA
    n = SUBSTEPS
    out_gas, out_lin = pl.pallas_call(
        kernel,
        out_shape=(
            pltpu.VMEM((NF, CH, BW, SEG), F32),
            pltpu.VMEM((NBLK, ARC, SEG), F32),
        ),
        in_specs=[hbm] * 11,
        out_specs=(pl.BlockSpec(memory_space=pltpu.VMEM),) * 2,
        scratch_shapes=[
            pltpu.VMEM((n, NF, CH + 2, 80, SEG), F32),
            pltpu.VMEM((n, NBLK, 48, SEG), F32),
            pltpu.VMEM((CH, BW, SEG), F32),
            pltpu.VMEM((CH, BW, SEG), F32),
            pltpu.VMEM((CH, BW, SEG), F32),
            pltpu.VMEM((n, NF, 8, SEG), F32),
            pltpu.VMEM((n, NF, 8, SEG), F32),
            pltpu.VMEM((n, NF, 8, SEG), F32),
            pltpu.VMEM((n, 3, 8, SEG), F32),
            pltpu.VMEM((n, 3, 8, SEG), F32),
            pltpu.VMEM((n, 3, 8, SEG), F32),
            pltpu.VMEM((n, NBLK, SEG), F32),
            pltpu.VMEM((n, NBLK, SEG), F32),
            pltpu.VMEM((n, NBLK, SEG), F32),
            pltpu.VMEM((n, NBLK, SEG), F32),
            pltpu.VMEM((n, 256, SEG), F32),
            pltpu.VMEM((NC, 8, SEG), F32),
            pltpu.VMEM((ROWS, 256), BF16),
            pltpu.VMEM((256, ROWS), BF16),
            pltpu.VMEM((ROWS, SEG), F32),
            pltpu.VMEM((ARC, 8 * NC), BF16),
            pltpu.VMEM((8 * NC, ARC), BF16),
            pltpu.VMEM((ARC, SEG), F32),
            pltpu.VMEM((NC, 16, SEG), F32),
            pltpu.VMEM((n, 8 * NC, SEG), F32),
            pltpu.VMEM((n, 8 * NC, SEG), F32),
            pltpu.VMEM((ROWS, SEG), F32),
            pltpu.VMEM((n, 8 * NC, SEG), F32),
            pltpu.VMEM((n, 256, SEG), F32),
            pltpu.VMEM((n, 8 * NC, SEG), F32),
            pltpu.VMEM((n, 2, ARC, SEG), F32),
            pltpu.VMEM((NF, CH, BW, SEG), F32),
            pltpu.VMEM((NBLK, ARC, SEG), F32),
            pltpu.VMEM((LD, ARC, SEG), F32),
            pltpu.SMEM((NF,), F32),
            pltpu.SMEM((NF,), F32),
            pltpu.SMEM((8,), F32),
            pltpu.SMEM((1,), jnp.int32),
            pltpu.VMEM((1, 256), jnp.int32),
            pltpu.VMEM((1, 256), F32),
            pltpu.VMEM((1, ROWS), jnp.int32),
            pltpu.VMEM((1, ROWS), jnp.int32),
            dma((n, NF, 2)), dma((n, NF, 2)),
            dma((n, NF, 2)), dma((n, NF, 2)),
            dma((n, 2)), dma((n, 2)),
            dma((n, 2)), dma((n, 2)),
            dma((n, NC - 1)), dma((n, NC - 1)),
            dma((n, NC - 1)), dma((n, NC - 1)),
            dma((NC - 1,)), dma((NC - 1,)),
            dma((15,)),
        ],
        compiler_params=pltpu.CompilerParams(
            collective_id=0, has_side_effects=True, vmem_limit_bytes=56 * 1024 * 1024
        ),
    )(
        gas, lin, velocity, diffusion, yields, rates,
        fire_cells.reshape(1, -1), release.reshape(1, -1),
        face_cells.reshape(1, -1), face_cycle.reshape(1, -1), face_count,
    )
    return leave(out_gas, out_lin, lining.shape)


def solution(mesh):
    in_specs = (
        P(None, "cross", None, "tunnel"),
        P(None, None, "cross", "tunnel"),
        P("cross", None, "tunnel"),
        P(), P(), P(), P(), P(),
        P(("tunnel", "cross")),
        P(("tunnel", "cross")),
        P(("tunnel", "cross")),
    )
    out_specs = (P(None, "cross", None, "tunnel"), P(None, None, "cross", "tunnel"))
    return jax.shard_map(on_device, mesh=mesh, in_specs=in_specs, out_specs=out_specs, check_vma=False)
```
